512 devices in a mesh: ctx: 32 (over z_lo, y), tp: 16 (over z_hi, x, core).
Axes of the slice: x: 4, y: 4, z: 16 (z_hi: 2, z_lo: 8; z = z_hi * 8 + z_lo), core: 2. Of those that a mesh axis runs over, the one named last changes fastest.
Arguments:
- branch_inputs: bfloat16 [3, 6144, 8192], P(None, 'ctx', 'tp'), may hold values from -6 to 6
- feat_taps: bfloat16 [3, 3, 8192], P(None, None, 'tp'), may hold values from -3.5 to 3.5
- long_filter: float32 [128, 8192], P(None, 'tp'), may hold values from -0.5 to 0.5
- out_weight: bfloat16 [8192, 8192], P('tp', 'ctx'), may hold values from -0.0625 to 0.0625
- cotangent: bfloat16 [6144, 8192], P(('ctx', 'tp')), may hold values from -6 to 6
Outputs:
- mixed_out: bfloat16 [6144, 8192], P(('ctx', 'tp'))
- grad_inputs: bfloat16 [3, 6144, 8192], P(None, 'ctx', 'tp')
- grad_filter: float32 [128, 8192], P(None, 'tp')
- grad_taps: float32 [3, 3, 8192], P(None, None, 'tp')
The draws below stay inside these ranges and needn't reach their ends.
All inputs are finite; a program needn't handle non-finite values.
Results may differ from the reference program's by a relative error of at most 0.03.
Values may be sent and summed in bfloat16 or wider, within the bound.
A program may use at most 64 MiB of HBM per device.

```python
import jax
import jax.numpy as jnp
from jax import lax

D = 8192
FILT = 128
FEAT = 3
TOKENS = 6144
N_TP = 16


def block_scale(own_key, dims, cuts, low, top_value):
    level = 1.0
    for axis_at, shards_of in cuts:
        heights = jax.random.uniform(jax.random.fold_in(jax.random.fold_in(own_key, 6), axis_at), (shards_of,), jnp.float32, low / len(cuts), top_value / len(cuts))
        level = level * jnp.repeat(jnp.exp(heights), dims[axis_at] // shards_of).reshape((-1,) + (1,) * (len(dims) - 1 - axis_at))
    return level


def normal_values(own_key, shape, width, limit, shards=(), dtype=jnp.bfloat16):
    level = block_scale(own_key, shape, shards, -0.22, 0.18) if shards else 1.0
    array = jax.random.normal(own_key, shape, jnp.float32) * width * level
    return jnp.minimum(jnp.maximum(array, -limit), limit).astype(dtype)


def setup_inputs(seed: int = 0) -> dict:
    splits = jax.random.split(jax.random.key(seed), 6)
    branch_inputs = normal_values(splits[0], (3, TOKENS, D), 1.0, 6.0, ((1, 32), (2, 16)))
    feat_taps = normal_values(splits[1], (3, FEAT, D), FEAT ** -0.5, 3.5, ((2, 16),))
    long_filter = normal_values(splits[2], (FILT, D), FILT ** -0.5, 0.5, ((1, 16),), jnp.float32)
    out_weight = normal_values(splits[3], (D, D), D ** -0.5, 0.0625, ((0, 16), (1, 32)))
    cotangent = normal_values(splits[4], (TOKENS, D), 1.0, 6.0, ((0, 512),))
    return dict(branch_inputs=branch_inputs, feat_taps=feat_taps, long_filter=long_filter, out_weight=out_weight, cotangent=cotangent)


def causal(signal, kernel):
    tap_total = kernel.shape[0]
    length = signal.shape[0]
    padded = jnp.concatenate([jnp.zeros((tap_total - 1, signal.shape[1]), jnp.float32), signal], axis=0)

    def add_tap(tap_index, running):
        window = lax.dynamic_slice_in_dim(padded, (tap_total - 1 - tap_index).astype(jnp.int32), length, 0)
        return running + kernel[tap_index] * window

    return lax.fori_loop(0, tap_total, add_tap, jnp.zeros(signal.shape, jnp.float32))


def anticausal(signal, kernel):
    tap_total = kernel.shape[0]
    length = signal.shape[0]
    padded = jnp.concatenate([signal, jnp.zeros((tap_total - 1, signal.shape[1]), jnp.float32)], axis=0)

    def add_tap(tap_index, running):
        window = lax.dynamic_slice_in_dim(padded, jnp.asarray(tap_index).astype(jnp.int32), length, 0)
        return running + kernel[tap_index] * window

    return lax.fori_loop(0, tap_total, add_tap, jnp.zeros(signal.shape, jnp.float32))


def correlate(gradient, values, tap_total):
    length = values.shape[0]
    padded = jnp.concatenate([jnp.zeros((tap_total - 1, values.shape[1]), jnp.float32), values], axis=0)

    def add_lag(lag_index, running):
        window = lax.dynamic_slice_in_dim(padded, (tap_total - 1 - lag_index).astype(jnp.int32), length, 0)
        column = jnp.sum(gradient * window, axis=0)[None]
        return lax.dynamic_update_slice_in_dim(running, column, jnp.asarray(lag_index).astype(jnp.int32), 0)

    return lax.fori_loop(0, tap_total, add_lag, jnp.zeros((tap_total, values.shape[1]), jnp.float32))


def reference(branch_inputs, feat_taps, long_filter, out_weight, cotangent):
    taps_wide = feat_taps.astype(jnp.float32)
    raw_wide = branch_inputs.astype(jnp.float32)
    featured = jnp.stack([causal(raw_wide[branch], taps_wide[branch]) for branch in range(3)]).astype(jnp.bfloat16)
    query_wide = featured[0].astype(jnp.float32)
    key_wide = featured[1].astype(jnp.float32)
    value_wide = featured[2].astype(jnp.float32)
    gated_pair = (key_wide * value_wide).astype(jnp.bfloat16)
    pair_wide = gated_pair.astype(jnp.float32)
    long_sum = causal(pair_wide, long_filter)
    gated_out = (query_wide * long_sum).astype(jnp.bfloat16)
    block_width = gated_out.shape[1] // N_TP
    running = jnp.zeros(cotangent.shape, jnp.float32)
    for block_index in range(N_TP):
        row_start = block_index * block_width
        block_out = jnp.dot(gated_out[:, row_start:row_start + block_width], out_weight[row_start:row_start + block_width],
                            preferred_element_type=jnp.float32).astype(jnp.bfloat16)
        running = running + lax.optimization_barrier(block_out).astype(jnp.float32)
    mixed_out = running.astype(jnp.bfloat16)
    grad_mixed = jnp.dot(cotangent, out_weight.T, preferred_element_type=jnp.float32)
    grad_long = grad_mixed * query_wide
    grad_pair = anticausal(grad_long, long_filter)
    grad_featured = jnp.stack([grad_mixed * long_sum, grad_pair * value_wide, grad_pair * key_wide])
    grad_inputs = jnp.stack([anticausal(grad_featured[branch], taps_wide[branch]) for branch in range(3)]).astype(jnp.bfloat16)
    grad_filter = correlate(grad_long, pair_wide, long_filter.shape[0])
    grad_taps = jnp.stack([correlate(grad_featured[branch], raw_wide[branch], feat_taps.shape[1]) for branch in range(3)])
    return mixed_out, grad_inputs, grad_filter, grad_taps
```

```python
import functools

import jax
import jax.numpy as jnp
from jax import lax
from jax.experimental import pallas as pl
from jax.experimental.pallas import tpu as pltpu
from jax.sharding import PartitionSpec as P

MESH = pl.DeviceIdType.MESH
NZ, NY, NX = 8, 4, 4


def coords():
    ctx = lax.axis_index("ctx")
    tp = lax.axis_index("tp")
    return ctx, tp, ctx // NY, ctx % NY, tp // (2 * NX), (tp // 2) % NX, tp % 2


def device(zl, y, zh, x, c):
    return {"ctx": zl * NY + y, "tp": zh * (2 * NX) + x * 2 + c}


def remote(src, dst, send, recv, target):
    return pltpu.make_async_remote_copy(
        src_ref=src, dst_ref=dst, send_sem=send, recv_sem=recv, device_id=target, device_id_type=MESH
    )


def greet(targets):
    barrier = pltpu.get_barrier_semaphore()
    count = 0
    for target, there in targets:
        if there is True:
            pl.semaphore_signal(barrier, inc=1, device_id=target, device_id_type=MESH)
            count = count + 1
        else:
            @pl.when(there)
            def _():
                pl.semaphore_signal(barrier, inc=1, device_id=target, device_id_type=MESH)

            count = count + there.astype(jnp.int32)
    pl.semaphore_wait(barrier, count)


def gather_kernel(
    w_ref, cot_ref, tail_ref, wg, cg, halo,
    own_sem, sib_s, sib_r, z_s, z_r, y_s, y_r, zp_s, zp_r, x_s, x_r, halo_s, halo_r,
):
    ctx, tp, zl, y, zh, x, c = coords()
    right = (zl + 1, y, zh, x, c)
    left = (zl - 1, y, zh, x, c)
    yp = device(zl, (y + 1) % NY, zh, x, c)
    ym = device(zl, (y + 3) % NY, zh, x, c)
    zpart = device(zl, y, 1 - zh, x, c)
    sib = device(zl, y, zh, x, 1 - c)
    xs = [device(zl, y, zh, (x + k) % NX, c) for k in (1, 2, 3)]
    nxt = {"ctx": jnp.minimum(ctx + 1, NZ * NY - 1), "tp": tp}
    prv = {"ctx": jnp.maximum(ctx - 1, 0), "tp": tp}
    dright = device(jnp.minimum(zl + 1, NZ - 1), y, zh, x, c)
    dleft = device(jnp.maximum(zl - 1, 0), y, zh, x, c)
    greet(
        [(sib, True), (yp, True), (ym, True), (zpart, True)]
        + [(d, True) for d in xs]
        + [(dright, zl < NZ - 1), (dleft, zl > 0), (nxt, ctx < NZ * NY - 1), (prv, ctx > 0)]
    )
    rows = w_ref.shape[0]

    def unit(zs, yy, h):
        return wg.at[zs * NY + yy, pl.ds(pl.multiple_of(h * rows, rows), rows)]

    keep = w_ref.at[:, pl.ds(pl.multiple_of(c * 128, 128), 128)]
    give = w_ref.at[:, pl.ds(pl.multiple_of((1 - c) * 128, 128), 128)]
    w_sib = remote(give, unit(zl, y, c), sib_s.at[0], sib_r.at[0], sib)
    w_sib.start()
    w_own = pltpu.make_async_copy(keep, unit(zl, y, c), own_sem.at[0])
    w_own.start()
    halo_copy = remote(tail_ref, halo, halo_s, halo_r, nxt)

    @pl.when(ctx < NZ * NY - 1)
    def _():
        halo_copy.start()

    c_sib = remote(cot_ref.at[1 - c], cg.at[tp], sib_s.at[1], sib_r.at[1], sib)
    c_sib.start()
    c_own = pltpu.make_async_copy(cot_ref.at[c], cg.at[tp], own_sem.at[1])
    c_own.start()

    def z_right(zs, h):
        return remote(unit(zs, y, h), unit(zs, y, h), z_s.at[0, zs, h], z_r.at[zs, h], dright)

    def z_left(zs, h):
        return remote(unit(zs, y, h), unit(zs, y, h), z_s.at[1, zs, h], z_r.at[zs, h], dleft)

    def y_plus(zs, yy, h, kind):
        return remote(unit(zs, yy, h), unit(zs, yy, h), y_s.at[kind, zs, h], y_r.at[kind, zs, h], yp)

    def y_minus(zs, yy, h, kind):
        return remote(unit(zs, yy, h), unit(zs, yy, h), y_s.at[kind, zs, h], y_r.at[kind, zs, h], ym)

    def spread(zs, h):
        y_plus(zs, y, h, 0).start()
        y_minus(zs, y, h, 1).start()

    def relay(zs, h):
        y_plus(zs, (y + 3) % NY, h, 0).wait_recv()
        y_minus(zs, (y + 1) % NY, h, 1).wait_recv()

        @pl.when(h == 0)
        def _():
            y_plus(zs, (y + 3) % NY, h, 2).start()

        @pl.when(h == 1)
        def _():
            y_minus(zs, (y + 1) % NY, h, 2).start()

    def cot_z(k):
        piece = zh * (2 * NX) + x * 2 + k
        return remote(cg.at[piece], cg.at[piece], zp_s.at[k], zp_r.at[k], zpart)

    def cot_x(half, k, n):
        piece = half * (2 * NX) + x * 2 + k
        return remote(cg.at[piece], cg.at[piece], x_s.at[half, k, n], x_r.at[half, k, n], xs[n])

    def cot_spread(half, k):
        for n in range(3):
            cot_x(half, k, n).start()

    c_own.wait()
    cot_z(c).start()
    cot_spread(zh, c)
    w_own.wait()
    order = (c, 1 - c)
    for step in range(NZ):
        for h in order:
            if step == 0:
                if h is not c:
                    w_sib.wait()

                @pl.when(zl < NZ - 1)
                def _(h=h):
                    z_right(zl, h).start()

                @pl.when(zl > 0)
                def _(h=h):
                    z_left(zl, h).start()

                spread(zl, h)
            else:
                @pl.when(zl - step >= 0)
                def _(h=h, step=step):
                    z_right(zl - step, h).wait_recv()

                    @pl.when(zl < NZ - 1)
                    def _():
                        z_right(zl - step, h).start()

                    spread(zl - step, h)

                @pl.when(zl + step < NZ)
                def _(h=h, step=step):
                    z_left(zl + step, h).wait_recv()

                    @pl.when(zl > 0)
                    def _():
                        z_left(zl + step, h).start()

                    spread(zl + step, h)
        if step == 0:
            c_sib.wait()
            cot_z(1 - c).start()
            cot_spread(zh, 1 - c)
        if step == 5:
            for k in order:
                cot_z(k).wait_recv()
                cot_spread(1 - zh, k)
        if step >= 1:
            for h in order:
                if step == 1:
                    relay(zl, h)
                else:
                    @pl.when(zl - step + 1 >= 0)
                    def _(h=h, step=step):
                        relay(zl - step + 1, h)

                    @pl.when(zl + step - 1 < NZ)
                    def _(h=h, step=step):
                        relay(zl + step - 1, h)
    for h in order:
        @pl.when(zl == NZ - 1)
        def _(h=h):
            relay(0, h)

        @pl.when(zl == 0)
        def _(h=h):
            relay(NZ - 1, h)

    @pl.loop(0, NZ)
    def _(zs):
        for h in (0, 1):
            y_plus(zs, (y + 2) % NY, h, 2).wait_recv()
            y_plus(zs, y, h, 0).wait_send()
            y_minus(zs, y, h, 1).wait_send()
            y_plus(zs, y, h, 2).wait_send()

            @pl.when((zs <= zl) & (zl < NZ - 1))
            def _():
                z_right(zs, h).wait_send()

            @pl.when((zs >= zl) & (zl > 0))
            def _():
                z_left(zs, h).wait_send()

    for k in (0, 1):
        cot_z(k).wait_send()
        for half in (0, 1):
            for n in range(3):
                cot_x(half, k, n).wait()

    @pl.when(ctx < NZ * NY - 1)
    def _():
        halo_copy.wait_send()

    @pl.when(ctx > 0)
    def _():
        halo_copy.wait_recv()


def gather(weight, cot, tail):
    rows = weight.shape[0]
    dma = pltpu.SemaphoreType.DMA
    any_space = pl.BlockSpec(memory_space=pl.ANY)
    vmem = pl.BlockSpec(memory_space=pltpu.VMEM)
    return pl.pallas_call(
        gather_kernel,
        out_shape=(
            jax.ShapeDtypeStruct((NZ * NY, 2 * rows, 128), jnp.bfloat16),
            jax.ShapeDtypeStruct((4 * NX,) + cot.shape[1:], jnp.bfloat16),
            jax.ShapeDtypeStruct(tail.shape, jnp.bfloat16),
        ),
        in_specs=[vmem, vmem, vmem],
        out_specs=(any_space, any_space, any_space),
        scratch_shapes=[
            dma((2,)), dma((2,)), dma((2,)),
            dma((2, NZ, 2)), dma((NZ, 2)), dma((3, NZ, 2)), dma((3, NZ, 2)),
            dma((2,)), dma((2,)), dma((2, 2, 3)), dma((2, 2, 3)),
            dma, dma,
        ],
        compiler_params=pltpu.CompilerParams(collective_id=0, has_side_effects=True),
        name="gather_weight_cotangent",
    )(weight, cot, tail)


def reduce_kernel(p_ref, o_ref, xbuf, zsend, zbuf, own, x_s, x_r, zp_s, zp_r, sib_s, sib_r):
    ctx, tp, zl, y, zh, x, c = coords()
    zpart = device(zl, y, 1 - zh, x, c)
    sib = device(zl, y, zh, x, 1 - c)
    xs = [device(zl, y, zh, (x + k) % NX, c) for k in (1, 2, 3)]
    greet([(sib, True), (zpart, True)] + [(d, True) for d in xs])
    half = p_ref.shape[2] // 2

    def to_x(zz, n, k):
        return remote(
            p_ref.at[zz, (x + n + 1) % NX, pl.ds(k * half, half)], xbuf.at[zz, n, pl.ds(k * half, half)],
            x_s.at[zz, n, k], x_r.at[zz, n, k], xs[n],
        )

    for zz in (1 - zh, zh):
        for k in (0, 1):
            for n in range(3):
                to_x(zz, n, k).start()

    def total(zz, k):
        for n in range(3):
            to_x(zz, n, k).wait_recv()
        rows = pl.ds(k * half, half)
        value = p_ref[zz, x, rows].astype(jnp.float32)
        for n in range(3):
            value = value + xbuf[zz, n, rows].astype(jnp.float32)
        return value

    def to_z(k):
        return remote(zsend.at[k], zbuf.at[k], zp_s.at[k], zp_r.at[k], zpart)

    for k in (0, 1):
        zsend[k] = total(1 - zh, k).astype(jnp.bfloat16)
        to_z(k).start()
    for k in (0, 1):
        own[k] = total(zh, k)
    for k in (0, 1):
        to_z(k).wait_recv()
        own[k] = own[k] + zbuf[k].astype(jnp.float32)
    to_z(0).wait_send()
    to_z(1).wait_send()
    zsend[0] = own[1 - c].astype(jnp.bfloat16)
    o_ref[c] = own[c].astype(jnp.bfloat16)
    last = remote(zsend.at[0], o_ref.at[c], sib_s, sib_r, sib)
    last.start()
    last.wait()
    for zz in (0, 1):
        for k in (0, 1):
            for n in range(3):
                to_x(zz, n, k).wait_send()


def reduce_out(partial):
    dma = pltpu.SemaphoreType.DMA
    rows, cols = partial.shape[2:]
    half = rows // 2
    vmem = pl.BlockSpec(memory_space=pltpu.VMEM)
    return pl.pallas_call(
        reduce_kernel,
        out_shape=jax.ShapeDtypeStruct((2, half, cols), jnp.bfloat16),
        in_specs=[vmem],
        out_specs=vmem,
        scratch_shapes=[
            pltpu.VMEM((2, 3, rows, cols), jnp.bfloat16),
            pltpu.VMEM((2, half, cols), jnp.bfloat16),
            pltpu.VMEM((2, half, cols), jnp.bfloat16),
            pltpu.VMEM((2, half, cols), jnp.float32),
            dma((2, 3, 2)), dma((2, 3, 2)), dma((2,)), dma((2,)), dma, dma,
        ],
        compiler_params=pltpu.CompilerParams(
            collective_id=1, has_side_effects=True, vmem_limit_bytes=32 * 2**20
        ),
        name="reduce_block_out",
    )(partial)


def sum_kernel(f_ref, o_ref, mine, ybuf, zbuf, y_s, y_r, z_s, z_r, t_s, t_r, g_s, g_r, e_s, e_r):
    ctx, tp, zl, y, zh, x, c = coords()
    ys = [device(zl, (y + k) % NY, zh, x, c) for k in (1, 2, 3)]
    zs = [device((zl + k) % NZ, y, zh, x, c) for k in range(1, NZ)]
    greet([(d, True) for d in ys + zs])

    def to_y(n):
        return remote(f_ref.at[(y + n + 1) % NY], ybuf.at[n], y_s.at[n], y_r.at[n], ys[n])

    def to_z(n):
        return remote(mine.at[(zl + n + 1) % NZ], zbuf.at[n, 0], z_s.at[n], z_r.at[n], zs[n])

    def taps_z(n):
        return remote(mine.at[NZ], zbuf.at[n, 1], t_s.at[n], t_r.at[n], zs[n])

    def back_z(n):
        return remote(o_ref.at[y, zl], o_ref.at[y, zl], g_s.at[n], g_r.at[n], zs[n])

    def back_y(n):
        return remote(o_ref.at[y], o_ref.at[y], e_s.at[n], e_r.at[n], ys[n])

    for n in range(3):
        to_y(n).start()
    value = f_ref[y].astype(jnp.float32)
    for n in range(3):
        to_y(n).wait_recv()
        value = value + ybuf[n].astype(jnp.float32)
    mine[...] = value.astype(jnp.bfloat16)
    for n in range(NZ - 1):
        to_z(n).start()
        taps_z(n).start()
    value = mine[zl].astype(jnp.float32)
    taps = mine[NZ].astype(jnp.float32)
    for n in range(NZ - 1):
        to_z(n).wait_recv()
        taps_z(n).wait_recv()
        value = value + zbuf[n, 0].astype(jnp.float32)
        taps = taps + zbuf[n, 1].astype(jnp.float32)
    o_ref[y, zl] = value.astype(jnp.bfloat16)
    o_ref[y, NZ] = taps.astype(jnp.bfloat16)
    for n in range(NZ - 1):
        back_z(n).start()
    for n in range(NZ - 1):
        back_z(n).wait()
    for n in range(3):
        back_y(n).start()
    for n in range(3):
        back_y(n).wait()
    for n in range(3):
        to_y(n).wait_send()
    for n in range(NZ - 1):
        to_z(n).wait_send()
        taps_z(n).wait_send()


def sum_gradients(parts):
    dma = pltpu.SemaphoreType.DMA
    vmem = pl.BlockSpec(memory_space=pltpu.VMEM)
    tile = parts.shape[1:]
    return pl.pallas_call(
        sum_kernel,
        out_shape=jax.ShapeDtypeStruct(parts.shape, jnp.bfloat16),
        in_specs=[vmem],
        out_specs=vmem,
        scratch_shapes=[
            pltpu.VMEM(tile, jnp.bfloat16),
            pltpu.VMEM((3,) + tile, jnp.bfloat16),
            pltpu.VMEM((NZ - 1, 2) + tile[1:], jnp.bfloat16),
            dma((3,)), dma((3,)), dma((NZ - 1,)), dma((NZ - 1,)), dma((NZ - 1,)), dma((NZ - 1,)),
            dma((NZ - 1,)), dma((NZ - 1,)), dma((3,)), dma((3,)),
        ],
        compiler_params=pltpu.CompilerParams(collective_id=2, has_side_effects=True),
        name="sum_filter_gradients",
    )(parts)


def from_behind(value, axis, steps):
    count = lax.axis_size(axis)
    first, last = (max(0, -steps), min(count, count - steps))
    return lax.ppermute(value, axis, [(source, source + steps) for source in range(first, last)])


def from_sibling(value):
    count = lax.axis_size("tp")
    return lax.ppermute(value, "tp", [(k, k ^ 1) for k in range(count)])


def depthwise(signal, kernel):
    result = lax.conv_general_dilated(
        signal[None],
        kernel[:, None, :],
        (1,),
        "VALID",
        dimension_numbers=("NWC", "WIO", "NWC"),
        feature_group_count=signal.shape[1],
        precision=lax.Precision.HIGHEST,
        preferred_element_type=jnp.float32,
    )
    return result[0]


def featurize(raw_rows, kernel_flip):
    return jax.vmap(depthwise)(raw_rows, kernel_flip).astype(jnp.bfloat16)


def body(branch_inputs, feat_taps, long_filter, out_weight, cotangent):
    tok_count = branch_inputs.shape[1]
    chan_count = branch_inputs.shape[2]
    tap_count = feat_taps.shape[1]
    filter_len = long_filter.shape[0]
    short_pad = tap_count - 1
    long_pad = filter_len - 1
    reach_len = long_pad + short_pad
    taps_flip = feat_taps[:, ::-1, :]
    filter_flip = long_filter[::-1]
    core = lax.axis_index("tp") % 2
    tail_rows = jnp.concatenate(
        [
            branch_inputs[0, tok_count - short_pad :],
            branch_inputs[1, tok_count - reach_len :],
            branch_inputs[2, tok_count - reach_len :],
            jnp.zeros((12, chan_count), jnp.bfloat16),
        ],
        axis=0,
    )
    own_rows = cotangent.shape[0]
    width = cotangent.shape[1]
    cot_halves = (
        cotangent.reshape(own_rows, 4, 8, 2, 128).transpose(3, 1, 0, 2, 4).reshape(2, 4 * own_rows, 1024)
    )
    weight_all, cot_all, arrived = gather(out_weight, cot_halves, tail_rows)
    arrived = jnp.where(lax.axis_index("ctx") > 0, arrived, jnp.zeros_like(arrived))
    query_head = arrived[:short_pad]
    key_head = arrived[short_pad : short_pad + reach_len]
    value_head = arrived[short_pad + reach_len : short_pad + 2 * reach_len]
    query_feat = featurize(
        jnp.concatenate([query_head, branch_inputs[0]], axis=0)[None], taps_flip[:1]
    )[0]
    key_value = jnp.stack(
        [
            jnp.concatenate([key_head, branch_inputs[1]], axis=0),
            jnp.concatenate([value_head, branch_inputs[2]], axis=0),
        ]
    )
    pair_feat = featurize(key_value, taps_flip[1:])
    pair_full = (pair_feat[0].astype(jnp.float32) * pair_feat[1].astype(jnp.float32)).astype(
        jnp.bfloat16
    )
    key_feat = pair_feat[0, long_pad:]
    value_feat = pair_feat[1, long_pad:]
    raw_heads = jnp.stack([query_head, key_head[long_pad:], value_head[long_pad:]])
    pair_wide = pair_full.astype(jnp.float32)
    long_sum = depthwise(pair_wide, filter_flip)
    query_wide = query_feat.astype(jnp.float32)
    gated_out = (query_wide * long_sum).astype(jnp.bfloat16)
    other_out = from_sibling(gated_out)
    both_out = jnp.where(
        core == 0,
        jnp.concatenate([gated_out, other_out], axis=1),
        jnp.concatenate([other_out, gated_out], axis=1),
    )
    product = jnp.einsum("tc,bcl->tbl", both_out, weight_all, preferred_element_type=jnp.float32)
    partial = (
        product.astype(jnp.bfloat16)
        .reshape(2, 4, 2, own_rows, 4, 1024)
        .transpose(0, 1, 2, 4, 3, 5)
        .reshape(2, 4, 8 * own_rows, 1024)
    )
    mixed = reduce_out(partial)
    mixed_out = mixed.reshape(2, 4, own_rows, 8, 128).transpose(2, 1, 3, 0, 4).reshape(own_rows, width)
    cot_half = cot_all.reshape(16, 4, own_rows, 8, 128).transpose(0, 2, 1, 3, 4).reshape(tok_count, 32, 128)
    grad_both = jnp.einsum("tbl,bcl->tc", cot_half, weight_all, preferred_element_type=jnp.float32)
    grad_own = lax.dynamic_slice_in_dim(grad_both, core * chan_count, chan_count, 1)
    grad_other = lax.dynamic_slice_in_dim(grad_both, (1 - core) * chan_count, chan_count, 1)
    grad_mixed = grad_own + from_sibling(grad_other)
    grad_long = grad_mixed * query_wide
    grad_query = grad_mixed * long_sum
    key_wide = key_feat.astype(jnp.float32)
    value_wide = value_feat.astype(jnp.float32)
    taps_wide = feat_taps.astype(jnp.float32)
    pair_lead = depthwise(grad_long[:reach_len], long_filter)
    head_rows = jnp.concatenate(
        [
            grad_long[:long_pad],
            grad_query[:short_pad],
            pair_lead * value_wide[:short_pad],
            pair_lead * key_wide[:short_pad],
        ],
        axis=0,
    )
    arrived_back = from_behind(head_rows.astype(jnp.bfloat16), "ctx", -1).astype(head_rows.dtype)
    grad_pair = depthwise(
        jnp.concatenate([grad_long, arrived_back[:long_pad]], axis=0), long_filter
    )
    grad_feat = jnp.stack([grad_query, grad_pair * value_wide, grad_pair * key_wide])
    feat_full = jnp.concatenate(
        [grad_feat, arrived_back[long_pad:].reshape(3, short_pad, chan_count)], axis=1
    )
    grad_in = jax.vmap(depthwise)(feat_full, taps_wide)
    filter_part = depthwise(pair_wide, grad_long)[::-1]
    raw_full = jnp.concatenate([raw_heads, branch_inputs], axis=1).astype(jnp.float32)
    taps_part = jax.vmap(depthwise)(raw_full, grad_feat)[:, ::-1, :]
    parts = jnp.concatenate(
        [filter_part, taps_part.reshape(9, chan_count), jnp.zeros((7, chan_count), jnp.float32)], axis=0
    ).astype(jnp.bfloat16)
    sums = sum_gradients(parts.reshape(9, 16, 4, 128).transpose(2, 0, 1, 3))
    sums = sums.transpose(1, 2, 0, 3).reshape(144, chan_count).astype(jnp.float32)
    grad_filter = sums[:filter_len]
    grad_taps = sums[filter_len : filter_len + 9].reshape(3, tap_count, chan_count)
    return (mixed_out, grad_in.astype(jnp.bfloat16), grad_filter, grad_taps)


def solution(mesh):
    placed = (
        P(None, "ctx", "tp"),
        P(None, None, "tp"),
        P(None, "tp"),
        P("tp", "ctx"),
        P(("ctx", "tp"), None),
    )
    return jax.shard_map(
        body,
        mesh=mesh,
        in_specs=placed,
        out_specs=(
            P(("ctx", "tp"), None),
            P(None, "ctx", "tp"),
            P(None, "tp"),
            P(None, None, "tp"),
        ),
        check_vma=False,
    )
```

```python
import functools

import jax
import jax.numpy as jnp
from jax import lax
from jax.experimental import pallas as pl
from jax.experimental.pallas import tpu as pltpu
from jax.sharding import PartitionSpec as P

MESH = pl.DeviceIdType.MESH
NZ, NY, NX = 8, 4, 4


def coords():
    ctx = lax.axis_index("ctx")
    tp = lax.axis_index("tp")
    return ctx, tp, ctx // NY, ctx % NY, tp // (2 * NX), (tp // 2) % NX, tp % 2


def device(zl, y, zh, x, c):
    return {"ctx": zl * NY + y, "tp": zh * (2 * NX) + x * 2 + c}


def remote(src, dst, send, recv, target):
    return pltpu.make_async_remote_copy(
        src_ref=src, dst_ref=dst, send_sem=send, recv_sem=recv, device_id=target, device_id_type=MESH
    )


def greet(targets):
    barrier = pltpu.get_barrier_semaphore()
    count = 0
    for target, there in targets:
        if there is True:
            pl.semaphore_signal(barrier, inc=1, device_id=target, device_id_type=MESH)
            count = count + 1
        else:
            @pl.when(there)
            def _():
                pl.semaphore_signal(barrier, inc=1, device_id=target, device_id_type=MESH)

            count = count + there.astype(jnp.int32)
    pl.semaphore_wait(barrier, count)


def block_kernel(
    w_ref, cot_ref, cotz_ref, x_ref, g_ref, s_ref,
    wg, cg, both, acc, out, arrived, gsend, grecv,
    own_sem, sib_s, sib_r, z_s, z_r, y_s, y_r, x_s, x_r, o_s, o_r,
):
    ctx, tp, zl, y, zh, x, c = coords()
    yp = device(zl, (y + 1) % NY, zh, x, c)
    ym = device(zl, (y + 3) % NY, zh, x, c)
    sib = device(zl, y, zh, x, 1 - c)
    xs = [device(zl, y, zh, (x + k) % NX, c) for k in (1, 2, 3)]
    dright = device(jnp.minimum(zl + 1, NZ - 1), y, zh, x, c)
    dleft = device(jnp.maximum(zl - 1, 0), y, zh, x, c)
    greet(
        [(sib, True), (yp, True), (ym, True)]
        + [(d, True) for d in xs]
        + [(dright, zl < NZ - 1), (dleft, zl > 0)]
    )
    rows = w_ref.shape[0]

    def unit(zs, yy, h):
        return wg.at[zs * NY + yy, pl.ds(pl.multiple_of(h * rows, rows), rows)]

    keep = w_ref.at[:, pl.ds(pl.multiple_of(c * 128, 128), 128)]
    give = w_ref.at[:, pl.ds(pl.multiple_of((1 - c) * 128, 128), 128)]
    w_sib = remote(give, unit(zl, y, c), sib_s.at[0], sib_r.at[0], sib)
    w_sib.start()
    w_own = pltpu.make_async_copy(keep, unit(zl, y, c), own_sem.at[0])
    w_own.start()
    x_sib = remote(x_ref, both.at[c], sib_s.at[1], sib_r.at[1], sib)
    x_sib.start()
    x_own = pltpu.make_async_copy(x_ref, both.at[c], own_sem.at[1])
    x_own.start()
    far = (1 - zh) * (2 * NX) + x * 2 + c
    c_sib = [
        remote(ref.at[1 - c], cg.at[at], sib_s.at[2 + n], sib_r.at[2 + n], sib)
        for n, (ref, at) in enumerate(((cot_ref, tp), (cotz_ref, far)))
    ]
    c_own = [
        pltpu.make_async_copy(ref.at[c], cg.at[at], own_sem.at[2 + n])
        for n, (ref, at) in enumerate(((cot_ref, tp), (cotz_ref, far)))
    ]
    for copy in c_sib + c_own:
        copy.start()

    def z_right(zs, h):
        return remote(unit(zs, y, h), unit(zs, y, h), z_s.at[0, zs, h], z_r.at[zs, h], dright)

    def z_left(zs, h):
        return remote(unit(zs, y, h), unit(zs, y, h), z_s.at[1, zs, h], z_r.at[zs, h], dleft)

    def y_plus(zs, yy, h, kind):
        return remote(unit(zs, yy, h), unit(zs, yy, h), y_s.at[kind, zs, h], y_r.at[kind, zs, h], yp)

    def y_minus(zs, yy, h, kind):
        return remote(unit(zs, yy, h), unit(zs, yy, h), y_s.at[kind, zs, h], y_r.at[kind, zs, h], ym)

    def spread(zs, h):
        y_plus(zs, y, h, 0).start()
        y_minus(zs, y, h, 1).start()

    def relay(zs, h):
        y_plus(zs, (y + 3) % NY, h, 0).wait_recv()
        y_minus(zs, (y + 1) % NY, h, 1).wait_recv()

        @pl.when(h == 0)
        def _():
            y_plus(zs, (y + 3) % NY, h, 2).start()

        @pl.when(h == 1)
        def _():
            y_minus(zs, (y + 1) % NY, h, 2).start()

    def cot_x(half, k, n):
        piece = half * (2 * NX) + x * 2 + k
        return remote(cg.at[piece], cg.at[piece], x_s.at[half, k, n], x_r.at[half, k, n], xs[n])

    def out_x(zs, n):
        return remote(out.at[zs, (x + n + 1) % NX], arrived.at[zs, n], o_s.at[zs, n], o_r.at[zs, n], xs[n])

    order = (c, 1 - c)
    w_own.wait()
    for h in order:
        if h is not c:
            w_sib.wait()

        @pl.when(zl < NZ - 1)
        def _(h=h):
            z_right(zl, h).start()

        @pl.when(zl > 0)
        def _(h=h):
            z_left(zl, h).start()

        spread(zl, h)
    for copy in c_own:
        copy.wait()
    for n in range(3):
        cot_x(zh, c, n).start()
        cot_x(1 - zh, c, n).start()
    for copy in c_sib:
        copy.wait()
    for n in range(3):
        cot_x(zh, 1 - c, n).start()
        cot_x(1 - zh, 1 - c, n).start()
    x_own.wait()
    x_sib.wait()
    acc[...] = jnp.zeros_like(acc)

    def weight(zs, k):
        return jnp.concatenate([wg[zs * NY + yy, k * rows : (k + 1) * rows] for yy in range(NY)], axis=1)

    def forward(zs):
        for h in (0, 1):
            y_plus(zs, (y + 2) % NY, h, 2).wait_recv()
        value = jnp.dot(both[0], weight(zs, 0), preferred_element_type=jnp.float32)
        value = value + jnp.dot(both[1], weight(zs, 1), preferred_element_type=jnp.float32)
        value = value.astype(jnp.bfloat16)
        for half in (0, 1):
            for xx in range(NX):
                at = (half * NX + xx) * 32
                out[zs, xx, half] = value[at : at + 32]
        for n in range(3):
            out_x(zs, n).start()

    def backward(zs):
        cot = jnp.concatenate([cg[piece, zs] for piece in range(4 * NX)], axis=0)
        for k in (0, 1):
            acc[k] += lax.dot_general(
                cot, weight(zs, k), (((1,), (1,)), ((), ())), preferred_element_type=jnp.float32
            )

    def collect(zs):
        value = out[zs, x].astype(jnp.float32)
        for n in range(3):
            out_x(zs, n).wait_recv()
            value = value + arrived[zs, n].astype(jnp.float32)
        value = value.astype(jnp.bfloat16)
        for half in (0, 1):
            for k in (0, 1):
                s_ref[half, k, zs] = value[half, k * 16 : (k + 1) * 16]

    def both_sides(step, act):
        @pl.loop(0, 2)
        def _(side):
            zs = zl + (2 * side - 1) * step

            @pl.when((step >= 0) & (zs >= 0) & (zs < NZ) & ((step > 0) | (side == 0)))
            def _():
                act(zs)

    @pl.loop(1, NZ + 2)
    def _(step):
        for h in order:
            @pl.when((zl - step >= 0) & (step < NZ))
            def _(h=h):
                z_right(zl - step, h).wait_recv()

                @pl.when(zl < NZ - 1)
                def _():
                    z_right(zl - step, h).start()

                spread(zl - step, h)

            @pl.when(zl + step < NZ)
            def _(h=h):
                z_left(zl + step, h).wait_recv()

                @pl.when(zl > 0)
                def _():
                    z_left(zl + step, h).start()

                spread(zl + step, h)

        def pass_on(zs):
            for h in order:
                relay(zs, h)

        both_sides(step - 1, pass_on)
        both_sides(step - 2, forward)
        both_sides(step - 4, collect)

        @pl.when(step == COT_STEP)
        def _():
            for k in (0, 1):
                for half in (0, 1):
                    for n in range(3):
                        cot_x(half, k, n).wait_recv()

        first = jnp.where(step < COT_STEP, 0, jnp.where(step == COT_STEP, 0, step - 2))
        last = jnp.where(step < COT_STEP, 0, step - 1)

        @pl.loop(first, last)
        def _(when):
            both_sides(when, backward)

    gsend[...] = acc[1 - c].astype(jnp.bfloat16)
    g_sib = remote(gsend, grecv, sib_s.at[4], sib_r.at[4], sib)
    g_sib.start()
    for step in (NZ - 2, NZ - 1):
        both_sides(jnp.int32(step), collect)
    g_sib.wait()
    g_ref[...] = acc[c] + grecv[...].astype(jnp.float32)

    @pl.loop(0, NZ)
    def _(zs):
        for h in (0, 1):
            y_plus(zs, y, h, 0).wait_send()
            y_minus(zs, y, h, 1).wait_send()
            y_plus(zs, y, h, 2).wait_send()

            @pl.when((zs <= zl) & (zl < NZ - 1))
            def _():
                z_right(zs, h).wait_send()

            @pl.when((zs >= zl) & (zl > 0))
            def _():
                z_left(zs, h).wait_send()

        for n in range(3):
            out_x(zs, n).wait_send()

    for k in (0, 1):
        for half in (0, 1):
            for n in range(3):
                cot_x(half, k, n).wait_send()


COT_STEP = 5


def project(weight, cot, cotz, gated):
    rows = weight.shape[0]
    dma = pltpu.SemaphoreType.DMA
    vmem = pl.BlockSpec(memory_space=pltpu.VMEM)
    toks = gated.shape[0]
    return pl.pallas_call(
        block_kernel,
        out_shape=(
            jax.ShapeDtypeStruct((toks, rows), jnp.float32),
            jax.ShapeDtypeStruct((2, 2, NZ, 16, 512), jnp.bfloat16),
        ),
        in_specs=[vmem] * 4,
        out_specs=(vmem, vmem),
        scratch_shapes=[
            pltpu.VMEM((NZ * NY, 2 * rows, 128), jnp.bfloat16),
            pltpu.VMEM((4 * NX, NZ, 16, 512), jnp.bfloat16),
            pltpu.VMEM((2, toks, rows), jnp.bfloat16),
            pltpu.VMEM((2, toks, rows), jnp.float32),
            pltpu.VMEM((NZ, NX, 2, 32, 512), jnp.bfloat16),
            pltpu.VMEM((NZ, 3, 2, 32, 512), jnp.bfloat16),
            pltpu.VMEM((toks, rows), jnp.bfloat16),
            pltpu.VMEM((toks, rows), jnp.bfloat16),
            dma((4,)), dma((5,)), dma((5,)),
            dma((2, NZ, 2)), dma((NZ, 2)), dma((3, NZ, 2)), dma((3, NZ, 2)),
            dma((2, 2, 3)), dma((2, 2, 3)), dma((NZ, 3)), dma((NZ, 3)),
        ],
        compiler_params=pltpu.CompilerParams(
            collective_id=0, has_side_effects=True, vmem_limit_bytes=40 * 2**20
        ),
        name="project_both_ways",
    )(weight, cot, cotz, gated)


def sum_kernel(
    f_ref, m_ref, o_ref, r_ref, mine, ybuf, zbuf, y_s, y_r, z_s, z_r, t_s, t_r, g_s, g_r, e_s, e_r, sib_s, sib_r
):
    ctx, tp, zl, y, zh, x, c = coords()
    ys = [device(zl, (y + k) % NY, zh, x, c) for k in (1, 2, 3)]
    zs = [device((zl + k) % NZ, y, zh, x, c) for k in range(1, NZ)]
    sib = device(zl, y, zh, x, 1 - c)
    greet([(sib, True)] + [(d, True) for d in ys + zs])
    m_sib = remote(m_ref.at[1 - c], r_ref.at[c], sib_s, sib_r, sib)

    def to_y(n):
        return remote(f_ref.at[(y + n + 1) % NY], ybuf.at[n], y_s.at[n], y_r.at[n], ys[n])

    def to_z(n):
        return remote(mine.at[(zl + n + 1) % NZ], zbuf.at[n, 0], z_s.at[n], z_r.at[n], zs[n])

    def taps_z(n):
        return remote(mine.at[NZ], zbuf.at[n, 1], t_s.at[n], t_r.at[n], zs[n])

    def back_z(n):
        return remote(o_ref.at[y, zl], o_ref.at[y, zl], g_s.at[n], g_r.at[n], zs[n])

    def back_y(n):
        return remote(o_ref.at[y], o_ref.at[y], e_s.at[n], e_r.at[n], ys[n])

    for n in range(3):
        to_y(n).start()
    m_sib.start()
    r_ref[c] = m_ref[c]
    value = f_ref[y].astype(jnp.float32)
    for n in range(3):
        to_y(n).wait_recv()
        value = value + ybuf[n].astype(jnp.float32)
    mine[...] = value.astype(jnp.bfloat16)
    for n in range(NZ - 1):
        to_z(n).start()
        taps_z(n).start()
    value = mine[zl].astype(jnp.float32)
    taps = mine[NZ].astype(jnp.float32)
    for n in range(NZ - 1):
        to_z(n).wait_recv()
        taps_z(n).wait_recv()
        value = value + zbuf[n, 0].astype(jnp.float32)
        taps = taps + zbuf[n, 1].astype(jnp.float32)
    o_ref[y, zl] = value.astype(jnp.bfloat16)
    o_ref[y, NZ] = taps.astype(jnp.bfloat16)
    for n in range(NZ - 1):
        back_z(n).start()
    for n in range(NZ - 1):
        back_z(n).wait()
    for n in range(3):
        back_y(n).start()
    for n in range(3):
        back_y(n).wait()
    for n in range(3):
        to_y(n).wait_send()
    for n in range(NZ - 1):
        to_z(n).wait_send()
        taps_z(n).wait_send()
    m_sib.wait()


def sum_gradients(parts, mixed):
    dma = pltpu.SemaphoreType.DMA
    vmem = pl.BlockSpec(memory_space=pltpu.VMEM)
    tile = parts.shape[1:]
    return pl.pallas_call(
        sum_kernel,
        out_shape=(
            jax.ShapeDtypeStruct(parts.shape, jnp.bfloat16),
            jax.ShapeDtypeStruct(mixed.shape, jnp.bfloat16),
        ),
        in_specs=[vmem, vmem],
        out_specs=(vmem, vmem),
        scratch_shapes=[
            pltpu.VMEM(tile, jnp.bfloat16),
            pltpu.VMEM((3,) + tile, jnp.bfloat16),
            pltpu.VMEM((NZ - 1, 2) + tile[1:], jnp.bfloat16),
            dma((3,)), dma((3,)), dma((NZ - 1,)), dma((NZ - 1,)), dma((NZ - 1,)), dma((NZ - 1,)),
            dma((NZ - 1,)), dma((NZ - 1,)), dma((3,)), dma((3,)), dma, dma,
        ],
        compiler_params=pltpu.CompilerParams(collective_id=2, has_side_effects=True),
        name="sum_filter_gradients",
    )(parts, mixed)


def from_behind(value, axis, steps):
    count = lax.axis_size(axis)
    first, last = (max(0, -steps), min(count, count - steps))
    return lax.ppermute(value, axis, [(source, source + steps) for source in range(first, last)])


def from_far(value):
    count = lax.axis_size("tp")
    return lax.ppermute(value, "tp", [(k, k ^ (count // 2)) for k in range(count)])


def depthwise(signal, kernel):
    result = lax.conv_general_dilated(
        signal[None],
        kernel[:, None, :],
        (1,),
        "VALID",
        dimension_numbers=("NWC", "WIO", "NWC"),
        feature_group_count=signal.shape[1],
        precision=lax.Precision.HIGHEST,
        preferred_element_type=jnp.float32,
    )
    return result[0]


def featurize(raw_rows, kernel_flip):
    return jax.vmap(depthwise)(raw_rows, kernel_flip).astype(jnp.bfloat16)


def body(branch_inputs, feat_taps, long_filter, out_weight, cotangent):
    tok_count = branch_inputs.shape[1]
    chan_count = branch_inputs.shape[2]
    tap_count = feat_taps.shape[1]
    filter_len = long_filter.shape[0]
    short_pad = tap_count - 1
    long_pad = filter_len - 1
    reach_len = long_pad + short_pad
    taps_flip = feat_taps[:, ::-1, :]
    filter_flip = long_filter[::-1]
    zhalf = lax.axis_index("tp") // (2 * NX)
    tail_rows = jnp.concatenate(
        [
            branch_inputs[0, tok_count - short_pad :],
            branch_inputs[1, tok_count - reach_len :],
            branch_inputs[2, tok_count - reach_len :],
        ],
        axis=0,
    )
    own_rows = cotangent.shape[0]
    width = cotangent.shape[1]
    cot_halves = jnp.pad(
        cotangent.reshape(own_rows, NZ, NY, 2, 128).transpose(3, 1, 0, 2, 4).reshape(2, NZ, own_rows, 512),
        ((0, 0), (0, 0), (0, 16 - own_rows), (0, 0)),
    )
    arrived = from_behind(tail_rows, "ctx", 1)
    cot_far = from_far(cot_halves)
    query_head = arrived[:short_pad]
    key_head = arrived[short_pad : short_pad + reach_len]
    value_head = arrived[short_pad + reach_len : short_pad + 2 * reach_len]
    query_feat = featurize(
        jnp.concatenate([query_head, branch_inputs[0]], axis=0)[None], taps_flip[:1]
    )[0]
    key_value = jnp.stack(
        [
            jnp.concatenate([key_head, branch_inputs[1]], axis=0),
            jnp.concatenate([value_head, branch_inputs[2]], axis=0),
        ]
    )
    pair_feat = featurize(key_value, taps_flip[1:])
    pair_full = (pair_feat[0].astype(jnp.float32) * pair_feat[1].astype(jnp.float32)).astype(
        jnp.bfloat16
    )
    key_feat = pair_feat[0, long_pad:]
    value_feat = pair_feat[1, long_pad:]
    raw_heads = jnp.stack([query_head, key_head[long_pad:], value_head[long_pad:]])
    pair_wide = pair_full.astype(jnp.float32)
    long_sum = depthwise(pair_wide, filter_flip)
    query_wide = query_feat.astype(jnp.float32)
    gated_out = (query_wide * long_sum).astype(jnp.bfloat16)
    gated_pad = jnp.pad(
        gated_out.reshape(16, own_rows, chan_count), ((0, 0), (0, 16 - own_rows), (0, 0))
    ).reshape(256, chan_count)
    grad_pad, out_sums = project(out_weight, cot_halves, cot_far, gated_pad)
    out_near = lax.dynamic_index_in_dim(out_sums, zhalf, 0, keepdims=False)
    out_far = from_far(lax.dynamic_index_in_dim(out_sums, 1 - zhalf, 0, keepdims=False))
    grad_mixed = grad_pad.reshape(16, 16, chan_count)[:, :own_rows].reshape(tok_count, chan_count)
    grad_long = grad_mixed * query_wide
    grad_query = grad_mixed * long_sum
    key_wide = key_feat.astype(jnp.float32)
    value_wide = value_feat.astype(jnp.float32)
    taps_wide = feat_taps.astype(jnp.float32)
    pair_lead = depthwise(grad_long[:reach_len], long_filter)
    head_rows = jnp.concatenate(
        [
            grad_long[:long_pad],
            grad_query[:short_pad],
            pair_lead * value_wide[:short_pad],
            pair_lead * key_wide[:short_pad],
        ],
        axis=0,
    )
    arrived_back = from_behind(head_rows.astype(jnp.bfloat16), "ctx", -1).astype(head_rows.dtype)
    grad_pair = depthwise(
        jnp.concatenate([grad_long, arrived_back[:long_pad]], axis=0), long_filter
    )
    grad_feat = jnp.stack([grad_query, grad_pair * value_wide, grad_pair * key_wide])
    feat_full = jnp.concatenate(
        [grad_feat, arrived_back[long_pad:].reshape(3, short_pad, chan_count)], axis=1
    )
    grad_in = jax.vmap(depthwise)(feat_full, taps_wide)
    filter_part = depthwise(pair_wide, grad_long)[::-1]
    raw_full = jnp.concatenate([raw_heads, branch_inputs], axis=1).astype(jnp.float32)
    taps_part = jax.vmap(depthwise)(raw_full, grad_feat)[:, ::-1, :]
    parts = jnp.concatenate(
        [filter_part, taps_part.reshape(9, chan_count), jnp.zeros((7, chan_count), jnp.float32)], axis=0
    ).astype(jnp.bfloat16)
    mixed = (out_near.astype(jnp.float32) + out_far.astype(jnp.float32)).astype(jnp.bfloat16)
    sums, mixed = sum_gradients(parts.reshape(9, 16, 4, 128).transpose(2, 0, 1, 3), mixed)
    mixed_out = (
        mixed[:, :, :own_rows].reshape(2, NZ, own_rows, NY, 128).transpose(2, 1, 3, 0, 4).reshape(own_rows, width)
    )
    sums = sums.transpose(1, 2, 0, 3).reshape(144, chan_count).astype(jnp.float32)
    grad_filter = sums[:filter_len]
    grad_taps = sums[filter_len : filter_len + 9].reshape(3, tap_count, chan_count)
    return (mixed_out, grad_in.astype(jnp.bfloat16), grad_filter, grad_taps)


def solution(mesh):
    placed = (
        P(None, "ctx", "tp"),
        P(None, None, "tp"),
        P(None, "tp"),
        P("tp", "ctx"),
        P(("ctx", "tp"), None),
    )
    return jax.shard_map(
        body,
        mesh=mesh,
        in_specs=placed,
        out_specs=(
            P(("ctx", "tp"), None),
            P(None, "ctx", "tp"),
            P(None, "tp"),
            P(None, None, "tp"),
        ),
        check_vma=False,
    )
```

```python
import functools

import jax
import jax.numpy as jnp
from jax import lax
from jax.experimental import pallas as pl
from jax.experimental.pallas import tpu as pltpu
from jax.sharding import PartitionSpec as P

MESH = pl.DeviceIdType.MESH
NZ, NY, NX = 8, 4, 4


def coords():
    ctx = lax.axis_index("ctx")
    tp = lax.axis_index("tp")
    return ctx, tp, ctx // NY, ctx % NY, tp // (2 * NX), (tp // 2) % NX, tp % 2


def device(zl, y, zh, x, c):
    return {"ctx": zl * NY + y, "tp": zh * (2 * NX) + x * 2 + c}


def remote(src, dst, send, recv, target):
    return pltpu.make_async_remote_copy(
        src_ref=src, dst_ref=dst, send_sem=send, recv_sem=recv, device_id=target, device_id_type=MESH
    )


def greet(targets):
    barrier = pltpu.get_barrier_semaphore()
    count = 0
    for target, there in targets:
        if there is True:
            pl.semaphore_signal(barrier, inc=1, device_id=target, device_id_type=MESH)
            count = count + 1
        else:
            @pl.when(there)
            def _():
                pl.semaphore_signal(barrier, inc=1, device_id=target, device_id_type=MESH)

            count = count + there.astype(jnp.int32)
    pl.semaphore_wait(barrier, count)


T = 192
PRE = 144
TAIL = 16
F32, BF16 = jnp.float32, jnp.bfloat16


def block_kernel(
    br_ref, taps_ref, fil_ref, w_ref, cot_ref,
    mixed_ref, gin_ref, gfil_ref, gtap_ref,
    wg, cp, cg, halo, qf, kf, vf, ls, rot, gated, both, acc, out, arrived, gsend, grecv,
    sums, far, near, come, other, glb, rg, gq, gk, gv, head, head_in, lead, lead_in, tg,
    part, mine, ybuf, zbuf, total, tpart, tmine, tybuf, tzbuf,
    own_sem, sib_s, sib_r, z_s, z_r, y_s, y_r, x_s, x_r, o_s, o_r, zp_s, zp_r, h_s, h_r,
    py_s, py_r, pz_s, pz_r, pt_s, pt_r, bz_s, bz_r, by_s, by_r, ty_s, ty_r,
):
    ctx, tp, zl, y, zh, x, c = coords()
    yp = device(zl, (y + 1) % NY, zh, x, c)
    ym = device(zl, (y + 3) % NY, zh, x, c)
    sib = device(zl, y, zh, x, 1 - c)
    zpart = device(zl, y, 1 - zh, x, c)
    xs = [device(zl, y, zh, (x + k) % NX, c) for k in (1, 2, 3)]
    ys = [device(zl, (y + k) % NY, zh, x, c) for k in (1, 2, 3)]
    zs_all = [device((zl + k) % NZ, y, zh, x, c) for k in range(1, NZ)]
    dright = device(jnp.minimum(zl + 1, NZ - 1), y, zh, x, c)
    dleft = device(jnp.maximum(zl - 1, 0), y, zh, x, c)
    last_ctx = NZ * NY - 1
    nxt = {"ctx": jnp.minimum(ctx + 1, last_ctx), "tp": tp}
    prv = {"ctx": jnp.maximum(ctx - 1, 0), "tp": tp}
    greet(
        [(sib, True), (zpart, True)]
        + [(d, True) for d in xs + ys + zs_all]
        + [(nxt, ctx < last_ctx), (prv, ctx > 0)]
    )
    rows = w_ref.shape[0]

    def unit(zs, yy, h):
        return wg.at[zs * NY + yy, pl.ds(pl.multiple_of(h * rows, rows), rows)]

    keep = w_ref.at[:, pl.ds(pl.multiple_of(c * 128, 128), 128)]
    give = w_ref.at[:, pl.ds(pl.multiple_of((1 - c) * 128, 128), 128)]
    w_sib = remote(give, unit(zl, y, c), sib_s.at[0], sib_r.at[0], sib)
    w_sib.start()
    w_own = pltpu.make_async_copy(keep, unit(zl, y, c), own_sem.at[0])
    w_own.start()
    c_sib = remote(cot_ref.at[1 - c], cp.at[tp], sib_s.at[1], sib_r.at[1], sib)
    c_sib.start()
    c_own = pltpu.make_async_copy(cot_ref.at[c], cp.at[tp], own_sem.at[1])
    c_own.start()
    halo_copies = [
        remote(br_ref.at[b, pl.ds(T - n, n)], halo.at[pl.ds(at, n)], h_s.at[b], h_r.at[b], nxt)
        for b, n, at in ((0, TAIL, 0), (1, PRE, TAIL), (2, PRE, TAIL + PRE))
    ]

    @pl.when(ctx < last_ctx)
    def _():
        for copy in halo_copies:
            copy.start()

    def z_right(zs, h):
        return remote(unit(zs, y, h), unit(zs, y, h), z_s.at[0, zs, h], z_r.at[zs, h], dright)

    def z_left(zs, h):
        return remote(unit(zs, y, h), unit(zs, y, h), z_s.at[1, zs, h], z_r.at[zs, h], dleft)

    def y_plus(zs, yy, h, kind):
        return remote(unit(zs, yy, h), unit(zs, yy, h), y_s.at[kind, zs, h], y_r.at[kind, zs, h], yp)

    def y_minus(zs, yy, h, kind):
        return remote(unit(zs, yy, h), unit(zs, yy, h), y_s.at[kind, zs, h], y_r.at[kind, zs, h], ym)

    def spread(zs, h):
        y_plus(zs, y, h, 0).start()
        y_minus(zs, y, h, 1).start()

    def relay(zs, h):
        y_plus(zs, (y + 3) % NY, h, 0).wait_recv()
        y_minus(zs, (y + 1) % NY, h, 1).wait_recv()

        @pl.when(h == 0)
        def _():
            y_plus(zs, (y + 3) % NY, h, 2).start()

        @pl.when(h == 1)
        def _():
            y_minus(zs, (y + 1) % NY, h, 2).start()

    def cot_z(k):
        piece = zh * (2 * NX) + x * 2 + k
        return remote(cp.at[piece], cp.at[piece], zp_s.at[k], zp_r.at[k], zpart)

    def cot_x(half, k, n):
        piece = half * (2 * NX) + x * 2 + k
        return remote(cp.at[piece], cp.at[piece], x_s.at[half, k, n], x_r.at[half, k, n], xs[n])

    def out_x(zs, n):
        return remote(out.at[zs, (x + n + 1) % NX], arrived.at[zs, n], o_s.at[zs, n], o_r.at[zs, n], xs[n])

    order = (c, 1 - c)
    w_own.wait()
    for h in order:
        if h is not c:
            w_sib.wait()

        @pl.when(zl < NZ - 1)
        def _(h=h):
            z_right(zl, h).start()

        @pl.when(zl > 0)
        def _(h=h):
            z_left(zl, h).start()

        spread(zl, h)
        if h is c:
            c_own.wait()
        else:
            c_sib.wait()
        cot_z(h).start()
        for n in range(3):
            cot_x(zh, h, n).start()
    acc[...] = jnp.zeros_like(acc)
    tg[...] = jnp.zeros_like(tg)

    @pl.when(ctx == 0)
    def _():
        halo[...] = jnp.zeros_like(halo)

    @pl.when(ctx == last_ctx)
    def _():
        head_in[...] = jnp.zeros_like(head_in)
        lead_in[...] = jnp.zeros_like(lead_in)

    def lane(l):
        return pl.ds(pl.multiple_of(l * 128, 128), 128)

    def spaced(value, count):
        shifted = pltpu.roll(value, value.shape[0] - 4, 0)
        for i in range(count):
            at = 12 * i
            yield (value[at : at + 16] if at % 8 == 0 else shifted[at - 4 : at + 12]).astype(BF16)

    def convolve(source, first, step, lanes):
        def residue(r, value):
            for q in range(16):
                tap = fil_ref[r, q : q + 1, lanes]
                value = value + tap * source(r, first + step * 8 * q)
            return value

        return lax.fori_loop(0, 8, residue, jnp.zeros((T, 128), F32))

    def features(l):
        lanes = lane(l)

        def feature(b, at, n):
            raw = jnp.concatenate([halo[at : at + n, lanes].astype(F32), br_ref[b, :, lanes].astype(F32)], axis=0)
            value = taps_ref[3 * b : 3 * b + 1, lanes] * raw
            for i in (1, 2):
                value = value + taps_ref[3 * b + i : 3 * b + i + 1, lanes] * pltpu.roll(raw, i, 0)
            return value.astype(BF16).astype(F32)

        query = feature(0, 0, TAIL)[TAIL:]
        key = feature(1, TAIL, PRE)
        value = feature(2, TAIL + PRE, PRE)
        qf[:, lanes] = query
        kf[:, lanes] = key[PRE:]
        vf[:, lanes] = value[PRE:]
        pair = (key * value).astype(BF16).astype(F32)
        rot[0, :, lanes] = pair
        for r in range(1, 8):
            rot[r, :, lanes] = pltpu.roll(pair, r, 0)
        long = convolve(lambda r, at: rot[r, pl.ds(at, T), lanes], PRE, -1, lanes)
        ls[:, lanes] = long
        for i, rows16 in enumerate(spaced(query * long, 16)):
            gated[16 * i : 16 * i + 16, lanes] = rows16

    def weight(zs, k):
        return jnp.concatenate([wg[zs * NY + yy, k * rows : (k + 1) * rows] for yy in range(NY)], axis=1)

    def forward(zs):
        value = jnp.dot(both[0], weight(zs, 0), preferred_element_type=F32)
        value = value + jnp.dot(both[1], weight(zs, 1), preferred_element_type=F32)
        value = value.astype(BF16)
        for half in (0, 1):
            for xx in range(NX):
                at = (half * NX + xx) * 32
                out[zs, xx, half] = value[at : at + 32]
        for n in range(3):
            out_x(zs, n).start()

    def backward(zs):
        for k in (0, 1):
            acc[k] += lax.dot_general(
                cg[zs], weight(zs, k), (((1,), (1,)), ((), ())), preferred_element_type=F32
            )

    def collect(zs):
        value = out[zs, x].astype(F32)
        for n in range(3):
            out_x(zs, n).wait_recv()
            value = value + arrived[zs, n].astype(F32)
        value = value.astype(BF16)
        for half in (0, 1):
            for k in (0, 1):
                sums[half, k, zs] = value[half, k * 16 : (k + 1) * 16]

    def both_sides(step, act):
        @pl.loop(0, 2)
        def _(side):
            zs = zl + (2 * side - 1) * step

            @pl.when((step >= 0) & (zs >= 0) & (zs < NZ) & ((step > 0) | (side == 0)))
            def _():
                act(zs)

    x_sib = remote(gated, both.at[c], sib_s.at[2], sib_r.at[2], sib)
    x_own = pltpu.make_async_copy(gated, both.at[c], own_sem.at[2])

    def forward_done(step):
        return jnp.maximum(0, jnp.minimum(2 * (step - 4), step - 1))

    def backward_done(step):
        return jnp.maximum(0, jnp.minimum(3 * (step - 5), step - 1))

    @pl.loop(1, NZ + 2)
    def _(step):
        for h in order:
            @pl.when((zl - step >= 0) & (step < NZ))
            def _(h=h):
                z_right(zl - step, h).wait_recv()

                @pl.when(zl < NZ - 1)
                def _():
                    z_right(zl - step, h).start()

                spread(zl - step, h)

            @pl.when(zl + step < NZ)
            def _(h=h):
                z_left(zl + step, h).wait_recv()

                @pl.when(zl > 0)
                def _():
                    z_left(zl + step, h).start()

                spread(zl + step, h)

        def pass_on(zs):
            for h in order:
                relay(zs, h)

        def relayed(zs):
            for h in (0, 1):
                y_plus(zs, (y + 2) % NY, h, 2).wait_recv()

        both_sides(step - 1, pass_on)
        both_sides(step - 2, relayed)

        @pl.when((step == 1) & (ctx > 0))
        def _():
            for copy in halo_copies:
                copy.wait_recv()

        @pl.when(step <= 4)
        def _():
            features(step - 1)

        @pl.when(step == 4)
        def _():
            x_sib.start()
            x_own.start()
            for k in order:
                cot_z(k).wait_recv()
                for n in range(3):
                    cot_x(1 - zh, k, n).start()

        @pl.when(step == 5)
        def _():
            x_own.wait()
            x_sib.wait()

        @pl.when(step == 6)
        def _():
            for k in (0, 1):
                for half in (0, 1):
                    for n in range(3):
                        cot_x(half, k, n).wait_recv()

            @pl.loop(0, 4 * NX)
            def _(piece):
                at = pl.ds(pl.multiple_of(piece * 16, 16), 16)
                for zs, rows16 in enumerate(spaced(cp[piece].astype(F32), NZ)):
                    cg[zs, at] = rows16

        @pl.loop(forward_done(step - 1), forward_done(step))
        def _(when):
            both_sides(when, forward)

        @pl.loop(backward_done(step - 1), backward_done(step))
        def _(when):
            both_sides(when, backward)

        @pl.loop(forward_done(step - 2), forward_done(step - 1))
        def _(when):
            both_sides(when, collect)

    gsend[...] = acc[1 - c].astype(BF16)
    g_sib = remote(gsend, grecv, sib_s.at[3], sib_r.at[3], sib)
    g_sib.start()
    both_sides(jnp.int32(NZ - 1), collect)
    out_far = remote(sums.at[1 - zh], far, zp_s.at[2], zp_r.at[2], zpart)
    out_far.start()
    g_sib.wait()

    def gradients(l):
        lanes = lane(l)
        low = lax.broadcasted_iota(jnp.int32, (8, 128), 0) < 4
        tiles = []
        for m in range(8):
            at = 32 * m
            block = acc[c, at : at + 32, lanes] + grecv[at : at + 32, lanes].astype(F32)
            up, down = pltpu.roll(block[16:24], 4, 0), pltpu.roll(block[24:32], 4, 0)
            tiles += [block[:8], jnp.where(low, block[8:16], up), jnp.where(low, up, down)]
        mixed_grad = jnp.concatenate(tiles, axis=0)
        long_grad = mixed_grad * qf[:, lanes]
        query_grad = mixed_grad * ls[:, lanes]
        glb[:T, lanes] = long_grad
        gq[:, lanes] = query_grad
        head[:128, lanes] = long_grad[:128].astype(BF16)
        head[128:, lanes] = query_grad[:TAIL].astype(BF16)

    @pl.loop(0, 4)
    def _(l):
        gradients(l)

    head_copy = remote(head, head_in, h_s.at[3], h_r.at[3], prv)

    @pl.when(ctx > 0)
    def _():
        head_copy.start()

    @pl.loop(0, 4)
    def _(l):
        lanes = lane(l)
        grad = glb[:T, lanes]

        @pl.loop(0, 8)
        def _(r):
            for q in range(16):
                total[r, q : q + 1, lanes] = jnp.sum(
                    grad * rot[r, pl.ds(PRE - 8 * q, T), lanes], axis=0, keepdims=True
                )

        for t in range(8):
            part[l, t] = total[t, :, lanes].astype(BF16)

    def to_y(n):
        return remote(part.at[(y + n + 1) % NY], ybuf.at[n], py_s.at[n], py_r.at[n], ys[n])

    def taps_y(n):
        return remote(tpart.at[(y + n + 1) % NY], tybuf.at[n], ty_s.at[n], ty_r.at[n], ys[n])

    def to_z(n):
        return remote(mine.at[(zl + n + 1) % NZ], zbuf.at[n], pz_s.at[n], pz_r.at[n], zs_all[n])

    def taps_z(n):
        return remote(tmine, tzbuf.at[n], pt_s.at[n], pt_r.at[n], zs_all[n])

    def back_z(n):
        return remote(other.at[y, zl], other.at[y, zl], bz_s.at[n], bz_r.at[n], zs_all[n])

    def back_y(n):
        return remote(other.at[y], other.at[y], by_s.at[n], by_r.at[n], ys[n])

    for n in range(3):
        to_y(n).start()

    @pl.when(ctx < last_ctx)
    def _():
        head_copy.wait_recv()

    @pl.loop(0, 4)
    def _(l):
        lanes = lane(l)
        glb[T:, lanes] = head_in[:128, lanes].astype(F32)
        full = glb[:, lanes]
        rg[0] = full
        for r in range(1, 8):
            rg[r] = pltpu.roll(full, full.shape[0] - r, 0)
        pair_grad = convolve(lambda r, at: rg[r, pl.ds(at, T)], 0, 1, lanes)
        key_grad = pair_grad * vf[:, lanes]
        value_grad = pair_grad * kf[:, lanes]
        gk[:, lanes] = key_grad
        gv[:, lanes] = value_grad
        lead[0, :, lanes] = key_grad[:TAIL].astype(BF16)
        lead[1, :, lanes] = value_grad[:TAIL].astype(BF16)
        for b, (at, grad) in enumerate(
            ((0, gq[:, lanes]), (PRE, key_grad), (2 * PRE, value_grad))
        ):
            raw = jnp.concatenate(
                [halo[at : at + TAIL, lanes].astype(F32), br_ref[b, :, lanes].astype(F32)], axis=0
            )
            for i in range(3):
                moved = raw if i == 0 else pltpu.roll(raw, i, 0)
                tg[3 * b + i : 3 * b + i + 1, lanes] = jnp.sum(grad * moved[TAIL:], axis=0, keepdims=True)
        tpart[l] = tg[:, lanes].astype(BF16)

    lead_copy = remote(lead, lead_in, h_s.at[4], h_r.at[4], prv)

    @pl.when(ctx > 0)
    def _():
        lead_copy.start()

    for n in range(3):
        taps_y(n).start()

    value = part[y].astype(F32)
    for n in range(3):
        to_y(n).wait_recv()
        value = value + ybuf[n].astype(F32)
    mine[...] = value.astype(BF16)
    for n in range(NZ - 1):
        to_z(n).start()

    @pl.when(ctx < last_ctx)
    def _():
        lead_copy.wait_recv()

    @pl.loop(0, 4)
    def _(l):
        lanes = lane(l)
        for b, (grad, ahead) in enumerate(
            ((gq, head_in[128:, lanes]), (gk, lead_in[0, :, lanes]), (gv, lead_in[1, :, lanes]))
        ):
            full = jnp.concatenate([grad[:, lanes], ahead.astype(F32)], axis=0)
            value = taps_ref[3 * b : 3 * b + 1, lanes] * full
            for i in (1, 2):
                value = value + taps_ref[3 * b + i : 3 * b + i + 1, lanes] * pltpu.roll(full, T + TAIL - i, 0)
            gin_ref[b, :, lanes] = value[:T].astype(BF16)

    value = tpart[y].astype(F32)
    for n in range(3):
        taps_y(n).wait_recv()
        value = value + tybuf[n].astype(F32)
    tmine[...] = value.astype(BF16)
    for n in range(NZ - 1):
        taps_z(n).start()
    value = mine[zl].astype(F32)
    for n in range(NZ - 1):
        to_z(n).wait_recv()
        value = value + zbuf[n].astype(F32)
    other[y, zl] = value.astype(BF16)
    for n in range(NZ - 1):
        back_z(n).start()

    out_far.wait()
    for k in (0, 1):
        near[k] = (sums[zh, k].astype(F32) + far[k].astype(F32)).astype(BF16)
    m_sib = remote(near.at[1 - c], come.at[c], sib_s.at[4], sib_r.at[4], sib)
    m_sib.start()

    value = tmine[...].astype(F32)
    for n in range(NZ - 1):
        taps_z(n).wait_recv()
        value = value + tzbuf[n].astype(F32)
    other[y, NZ] = value.astype(BF16)
    for n in range(NZ - 1):
        back_z(n).wait()
    for n in range(3):
        back_y(n).start()
    m_sib.wait()
    for k in (0, 1):
        for zs in range(NZ):
            for yy in range(NY):
                at = (zs * NY + yy) * 256
                lanes = slice(yy * 128, (yy + 1) * 128)

                @pl.when(c == k)
                def _(zs=zs, lanes=lanes, at=at, k=k):
                    mixed_ref[:, at + k * 128 : at + (k + 1) * 128] = near[k, zs, :, lanes][:12]

                @pl.when(c != k)
                def _(zs=zs, lanes=lanes, at=at, k=k):
                    mixed_ref[:, at + k * 128 : at + (k + 1) * 128] = come[k, zs, :, lanes][:12]

    for n in range(3):
        back_y(n).wait()
    for l in range(4):
        for t in range(8):
            gfil_ref[t, :, l * 128 : (l + 1) * 128] = other[l, t].astype(F32)
        gtap_ref[:, l * 128 : (l + 1) * 128] = other[l, NZ].astype(F32)
    for n in range(3):
        to_y(n).wait_send()
        taps_y(n).wait_send()
    for n in range(NZ - 1):
        to_z(n).wait_send()
        taps_z(n).wait_send()

    @pl.when(ctx > 0)
    def _():
        head_copy.wait_send()
        lead_copy.wait_send()

    @pl.when(ctx < last_ctx)
    def _():
        for copy in halo_copies:
            copy.wait_send()

    @pl.loop(0, NZ)
    def _(zs):
        for h in (0, 1):
            y_plus(zs, y, h, 0).wait_send()
            y_minus(zs, y, h, 1).wait_send()
            y_plus(zs, y, h, 2).wait_send()

            @pl.when((zs <= zl) & (zl < NZ - 1))
            def _():
                z_right(zs, h).wait_send()

            @pl.when((zs >= zl) & (zl > 0))
            def _():
                z_left(zs, h).wait_send()

        for n in range(3):
            out_x(zs, n).wait_send()

    for k in (0, 1):
        cot_z(k).wait_send()
        for half in (0, 1):
            for n in range(3):
                cot_x(half, k, n).wait_send()


def block(branches, taps, filt, weight, cot):
    rows = weight.shape[0]
    wide = branches.shape[2]
    dma = pltpu.SemaphoreType.DMA
    vmem = pl.BlockSpec(memory_space=pltpu.VMEM)

    def f32(*shape):
        return pltpu.VMEM(shape, F32)

    def b16(*shape):
        return pltpu.VMEM(shape, BF16)

    return pl.pallas_call(
        block_kernel,
        out_shape=(
            jax.ShapeDtypeStruct((12, 8192), BF16),
            jax.ShapeDtypeStruct(branches.shape, BF16),
            jax.ShapeDtypeStruct(filt.shape, F32),
            jax.ShapeDtypeStruct((16, wide), F32),
        ),
        in_specs=[vmem] * 5,
        out_specs=(vmem,) * 4,
        scratch_shapes=[
            b16(NZ * NY, 2 * rows, 128), b16(4 * NX, 96, 512), b16(NZ, 256, 512), b16(TAIL + 2 * PRE, wide),
            f32(T, wide), f32(T, wide), f32(T, wide), f32(T, wide), f32(8, T + PRE, wide),
            b16(256, wide), b16(2, 256, wide), f32(2, 256, wide),
            b16(NZ, NX, 2, 32, 512), b16(NZ, 3, 2, 32, 512), b16(256, wide), b16(256, wide),
            b16(2, 2, NZ, 16, 512), b16(2, NZ, 16, 512), b16(2, NZ, 16, 512), b16(2, NZ, 16, 512),
            b16(NY, NZ + 1, 16, 128),
            f32(T + 128, wide), f32(8, T + 128, 128), f32(T, wide), f32(T, wide), f32(T, wide),
            b16(128 + TAIL, wide), b16(128 + TAIL, wide), b16(2, TAIL, wide), b16(2, TAIL, wide), f32(16, wide),
            b16(NY, NZ, 16, 128), b16(NZ, 16, 128), b16(3, NZ, 16, 128), b16(NZ - 1, 16, 128), f32(8, 16, wide),
            b16(NY, 16, 128), b16(16, 128), b16(3, 16, 128), b16(NZ - 1, 16, 128),
            dma((3,)), dma((5,)), dma((5,)),
            dma((2, NZ, 2)), dma((NZ, 2)), dma((3, NZ, 2)), dma((3, NZ, 2)),
            dma((2, 2, 3)), dma((2, 2, 3)), dma((NZ, 3)), dma((NZ, 3)), dma((3,)), dma((3,)), dma((5,)), dma((5,)),
            dma((3,)), dma((3,)), dma((NZ - 1,)), dma((NZ - 1,)), dma((NZ - 1,)), dma((NZ - 1,)),
            dma((NZ - 1,)), dma((NZ - 1,)), dma((3,)), dma((3,)), dma((3,)), dma((3,)),
        ],
        compiler_params=pltpu.CompilerParams(
            collective_id=0, has_side_effects=True, vmem_limit_bytes=56 * 2**20
        ),
        name="hyena_block",
    )(branches, taps, filt, weight, cot)


def body(branch_inputs, feat_taps, long_filter, out_weight, cotangent):
    own_rows = cotangent.shape[0]
    chan_count = branch_inputs.shape[2]
    tap_count = feat_taps.shape[1]
    cot_halves = (
        cotangent.reshape(own_rows, NZ, NY, 2, 128).transpose(3, 1, 0, 2, 4).reshape(2, NZ * own_rows, 512)
    )
    taps = feat_taps.astype(F32).reshape(3 * tap_count, chan_count)
    filt = long_filter.reshape(16, 8, chan_count).transpose(1, 0, 2)
    mixed_out, grad_inputs, grad_filter, grad_taps = block(branch_inputs, taps, filt, out_weight, cot_halves)
    grad_filter = grad_filter.transpose(1, 0, 2).reshape(long_filter.shape)
    return mixed_out, grad_inputs, grad_filter, grad_taps[:9].reshape(3, tap_count, chan_count)


def solution(mesh):
    placed = (
        P(None, "ctx", "tp"),
        P(None, None, "tp"),
        P(None, "tp"),
        P("tp", "ctx"),
        P(("ctx", "tp"), None),
    )
    return jax.shard_map(
        body,
        mesh=mesh,
        in_specs=placed,
        out_specs=(
            P(("ctx", "tp"), None),
            P(None, "ctx", "tp"),
            P(None, "tp"),
            P(None, None, "tp"),
        ),
        check_vma=False,
    )
```

```python
import functools

import jax
import jax.numpy as jnp
from jax import lax
from jax.experimental import pallas as pl
from jax.experimental.pallas import tpu as pltpu
from jax.sharding import PartitionSpec as P

MESH = pl.DeviceIdType.MESH
NZ, NY, NX = 8, 4, 4


def coords():
    ctx = lax.axis_index("ctx")
    tp = lax.axis_index("tp")
    return ctx, tp, ctx // NY, ctx % NY, tp // (2 * NX), (tp // 2) % NX, tp % 2


def device(zl, y, zh, x, c):
    return {"ctx": zl * NY + y, "tp": zh * (2 * NX) + x * 2 + c}


def remote(src, dst, send, recv, target):
    return pltpu.make_async_remote_copy(
        src_ref=src, dst_ref=dst, send_sem=send, recv_sem=recv, device_id=target, device_id_type=MESH
    )


def greet(targets):
    barrier = pltpu.get_barrier_semaphore()
    count = 0
    for target, there in targets:
        if there is True:
            pl.semaphore_signal(barrier, inc=1, device_id=target, device_id_type=MESH)
            count = count + 1
        else:
            @pl.when(there)
            def _():
                pl.semaphore_signal(barrier, inc=1, device_id=target, device_id_type=MESH)

            count = count + there.astype(jnp.int32)
    pl.semaphore_wait(barrier, count)


T = 192
PRE = 144
TAIL = 16
F32, BF16 = jnp.float32, jnp.bfloat16


def block_kernel(
    br_ref, ftaps_ref, filt_ref, w_ref, cot_ref,
    mixed_ref, gin_ref, gfil_ref, gtap_ref,
    taps_ref, fil_ref, wg, cp, cg, halo, qf, kf, vf, ls, rot, gated, both, acc, out, arrived, gsend, grecv,
    sums, far, near, come, other, glb, rg, gq, gk, gv, head, head_in, lead, lead_in, tg,
    part, mine, ybuf, zbuf, total, tpart, tmine, tybuf, tzbuf,
    own_sem, sib_s, sib_r, z_s, z_r, y_s, y_r, x_s, x_r, o_s, o_r, zp_s, zp_r, f_s, f_r, h_s, h_r,
    py_s, py_r, pz_s, pz_r, pt_s, pt_r, bz_s, bz_r, by_s, by_r, ty_s, ty_r,
):
    ctx, tp, zl, y, zh, x, c = coords()
    yp = device(zl, (y + 1) % NY, zh, x, c)
    ym = device(zl, (y + 3) % NY, zh, x, c)
    sib = device(zl, y, zh, x, 1 - c)
    zpart = device(zl, y, 1 - zh, x, c)
    xs = [device(zl, y, zh, (x + k) % NX, c) for k in (1, 2, 3)]
    ys = [device(zl, (y + k) % NY, zh, x, c) for k in (1, 2, 3)]
    zs_all = [device((zl + k) % NZ, y, zh, x, c) for k in range(1, NZ)]
    dright = device(jnp.minimum(zl + 1, NZ - 1), y, zh, x, c)
    dleft = device(jnp.maximum(zl - 1, 0), y, zh, x, c)
    last_ctx = NZ * NY - 1
    nxt = {"ctx": jnp.minimum(ctx + 1, last_ctx), "tp": tp}
    prv = {"ctx": jnp.maximum(ctx - 1, 0), "tp": tp}
    greet(
        [(sib, True), (zpart, True)]
        + [(d, True) for d in xs + ys + zs_all]
        + [(nxt, ctx < last_ctx), (prv, ctx > 0)]
    )
    rows = w_ref.shape[0]

    def unit(zs, yy, h):
        return wg.at[zs * NY + yy, pl.ds(pl.multiple_of(h * rows, rows), rows)]

    keep = w_ref.at[:, pl.ds(pl.multiple_of(c * 128, 128), 128)]
    give = w_ref.at[:, pl.ds(pl.multiple_of((1 - c) * 128, 128), 128)]
    w_sib = remote(give, unit(zl, y, c), sib_s.at[0], sib_r.at[0], sib)
    w_sib.start()
    w_own = pltpu.make_async_copy(keep, unit(zl, y, c), own_sem.at[0])
    w_own.start()
    c_sib = remote(cot_ref.at[1 - c], cp.at[tp], sib_s.at[1], sib_r.at[1], sib)
    c_sib.start()
    c_own = pltpu.make_async_copy(cot_ref.at[c], cp.at[tp], own_sem.at[1])
    c_own.start()
    halo_copies = [
        remote(br_ref.at[b, pl.ds(T - n, n)], halo.at[pl.ds(at, n)], h_s.at[b], h_r.at[b], nxt)
        for b, n, at in ((0, TAIL, 0), (1, PRE, TAIL), (2, PRE, TAIL + PRE))
    ]

    @pl.when(ctx < last_ctx)
    def _():
        for copy in halo_copies:
            copy.start()

    def z_right(zs, h):
        return remote(unit(zs, y, h), unit(zs, y, h), z_s.at[0, zs, h], z_r.at[zs, h], dright)

    def z_left(zs, h):
        return remote(unit(zs, y, h), unit(zs, y, h), z_s.at[1, zs, h], z_r.at[zs, h], dleft)

    def y_plus(zs, yy, h, kind):
        return remote(unit(zs, yy, h), unit(zs, yy, h), y_s.at[kind, zs, h], y_r.at[kind, zs, h], yp)

    def y_minus(zs, yy, h, kind):
        return remote(unit(zs, yy, h), unit(zs, yy, h), y_s.at[kind, zs, h], y_r.at[kind, zs, h], ym)

    def spread(zs, h):
        y_plus(zs, y, h, 0).start()
        y_minus(zs, y, h, 1).start()

    def relay(zs, h):
        y_plus(zs, (y + 3) % NY, h, 0).wait_recv()
        y_minus(zs, (y + 1) % NY, h, 1).wait_recv()

        @pl.when(h == 0)
        def _():
            y_plus(zs, (y + 3) % NY, h, 2).start()

        @pl.when(h == 1)
        def _():
            y_minus(zs, (y + 1) % NY, h, 2).start()

    def cot_z(k):
        piece = zh * (2 * NX) + x * 2 + k
        return remote(cp.at[piece], cp.at[piece], zp_s.at[k], zp_r.at[k], zpart)

    def cot_x(half, k, n):
        piece = half * (2 * NX) + x * 2 + k
        return remote(cp.at[piece], cp.at[piece], x_s.at[half, k, n], x_r.at[half, k, n], xs[n])

    def out_x(zs, n):
        return remote(out.at[zs, (x + n + 1) % NX], arrived.at[zs, n], o_s.at[zs, n], o_r.at[zs, n], xs[n])

    order = (c, 1 - c)
    w_own.wait()
    for h in order:
        if h is not c:
            w_sib.wait()

        @pl.when(zl < NZ - 1)
        def _(h=h):
            z_right(zl, h).start()

        @pl.when(zl > 0)
        def _(h=h):
            z_left(zl, h).start()

        spread(zl, h)
        if h is c:
            c_own.wait()
        else:
            c_sib.wait()
        cot_z(h).start()
        for n in range(3):
            cot_x(zh, h, n).start()
    for b in range(3):
        taps_ref[b] = ftaps_ref[b].astype(F32)
    for j in range(128):
        fil_ref[j % 8, j // 8 : j // 8 + 1] = filt_ref[j : j + 1]
    acc[...] = jnp.zeros_like(acc)
    tg[...] = jnp.zeros_like(tg)

    @pl.when(ctx == 0)
    def _():
        halo[...] = jnp.zeros_like(halo)

    @pl.when(ctx == last_ctx)
    def _():
        head_in[...] = jnp.zeros_like(head_in)
        lead_in[...] = jnp.zeros_like(lead_in)

    def lane(l):
        return pl.ds(pl.multiple_of(l * 128, 128), 128)

    def spaced(value, count):
        shifted = pltpu.roll(value, value.shape[0] - 4, 0)
        for i in range(count):
            at = 12 * i
            yield (value[at : at + 16] if at % 8 == 0 else shifted[at - 4 : at + 12]).astype(BF16)

    def convolve(source, first, step, lanes):
        def residue(r, value):
            for q in range(16):
                tap = fil_ref[r, q : q + 1, lanes]
                value = value + tap * source(r, first + step * 8 * q)
            return value

        return lax.fori_loop(0, 8, residue, jnp.zeros((T, 128), F32))

    def features(l):
        lanes = lane(l)

        def feature(b, at, n):
            raw = jnp.concatenate([halo[at : at + n, lanes].astype(F32), br_ref[b, :, lanes].astype(F32)], axis=0)
            value = taps_ref[b, 0:1, lanes] * raw
            for i in (1, 2):
                value = value + taps_ref[b, i : i + 1, lanes] * pltpu.roll(raw, i, 0)
            return value.astype(BF16).astype(F32)

        query = feature(0, 0, TAIL)[TAIL:]
        key = feature(1, TAIL, PRE)
        value = feature(2, TAIL + PRE, PRE)
        qf[:, lanes] = query
        kf[:, lanes] = key[PRE:]
        vf[:, lanes] = value[PRE:]
        pair = (key * value).astype(BF16).astype(F32)
        rot[0, :, lanes] = pair
        for r in range(1, 8):
            rot[r, :, lanes] = pltpu.roll(pair, r, 0)
        long = convolve(lambda r, at: rot[r, pl.ds(at, T), lanes], PRE, -1, lanes)
        ls[:, lanes] = long
        for i, rows16 in enumerate(spaced(query * long, 16)):
            gated[16 * i : 16 * i + 16, lanes] = rows16

    def weight(zs, k):
        return jnp.concatenate([wg[zs * NY + yy, k * rows : (k + 1) * rows] for yy in range(NY)], axis=1)

    def forward(zs):
        value = jnp.dot(both[0], weight(zs, 0), preferred_element_type=F32)
        value = value + jnp.dot(both[1], weight(zs, 1), preferred_element_type=F32)
        value = value.astype(BF16)
        for half in (0, 1):
            for xx in range(NX):
                at = (half * NX + xx) * 32
                out[zs, xx, half] = value[at : at + 32]
        for n in range(3):
            out_x(zs, n).start()

    def backward(zs):
        for k in (0, 1):
            acc[k] += lax.dot_general(
                cg[zs], weight(zs, k), (((1,), (1,)), ((), ())), preferred_element_type=F32
            )

    def collect(zs):
        value = out[zs, x].astype(F32)
        for n in range(3):
            out_x(zs, n).wait_recv()
            value = value + arrived[zs, n].astype(F32)
        value = value.astype(BF16)
        for half in (0, 1):
            for k in (0, 1):
                sums[half, zs, k] = value[half, k * 16 : (k + 1) * 16]

    near_end = jnp.minimum(zl, NZ - 1 - zl)

    def nth(n):
        paired = jnp.where(n % 2 == 1, zl - (n + 1) // 2, zl + n // 2)
        single = jnp.where(zl < NZ // 2, zl + (n - near_end), zl - (n - near_end))
        return jnp.where(n <= 2 * near_end, paired, single)

    def each(first, last, act):
        @pl.loop(first, last)
        def _(n):
            act(nth(n))

    x_sib = remote(gated, both.at[c], sib_s.at[2], sib_r.at[2], sib)
    x_own = pltpu.make_async_copy(gated, both.at[c], own_sem.at[2])

    def forward_done(step):
        return jnp.maximum(0, jnp.minimum(2 * (step - 4), step - 1))

    def backward_done(step):
        return jnp.maximum(0, jnp.minimum(3 * (step - 5), step - 1))

    @pl.loop(1, NZ + 2)
    def _(step):
        for h in order:
            @pl.when((zl - step >= 0) & (step < NZ))
            def _(h=h):
                z_right(zl - step, h).wait_recv()

                @pl.when(zl < NZ - 1)
                def _():
                    z_right(zl - step, h).start()

                spread(zl - step, h)

            @pl.when(zl + step < NZ)
            def _(h=h):
                z_left(zl + step, h).wait_recv()

                @pl.when(zl > 0)
                def _():
                    z_left(zl + step, h).start()

                spread(zl + step, h)

        def pass_on(zs):
            for h in order:
                relay(zs, h)

        def relayed(zs):
            for h in (0, 1):
                y_plus(zs, (y + 2) % NY, h, 2).wait_recv()

        @pl.when(step <= NZ)
        def _():
            pass_on(nth(step - 1))

        @pl.when(step >= 2)
        def _():
            relayed(nth(step - 2))

        @pl.when((step == 1) & (ctx > 0))
        def _():
            for copy in halo_copies:
                copy.wait_recv()

        @pl.when(step <= 4)
        def _():
            features(step - 1)

        @pl.when(step == 4)
        def _():
            x_sib.start()
            x_own.start()
            for k in order:
                cot_z(k).wait_recv()
                for n in range(3):
                    cot_x(1 - zh, k, n).start()

        @pl.when(step == 5)
        def _():
            x_own.wait()
            x_sib.wait()

        @pl.when(step == 6)
        def _():
            for k in (0, 1):
                for half in (0, 1):
                    for n in range(3):
                        cot_x(half, k, n).wait_recv()

            @pl.loop(0, 4 * NX)
            def _(piece):
                at = pl.ds(pl.multiple_of(piece * 16, 16), 16)
                for zs, rows16 in enumerate(spaced(cp[piece].astype(F32), NZ)):
                    cg[zs, at] = rows16

        each(forward_done(step - 1), forward_done(step), forward)
        each(backward_done(step - 1), backward_done(step), backward)
        each(forward_done(step - 3), forward_done(step - 2), collect)

    gsend[...] = acc[1 - c].astype(BF16)
    g_sib = remote(gsend, grecv, sib_s.at[3], sib_r.at[3], sib)
    g_sib.start()

    def out_far(zs):
        return remote(sums.at[1 - zh, zs], far.at[zs], f_s.at[zs], f_r.at[zs], zpart)

    done = forward_done(NZ - 1)
    each(0, done, lambda zs: out_far(zs).start())
    g_sib.wait()

    def gradients(l):
        lanes = lane(l)
        low = lax.broadcasted_iota(jnp.int32, (8, 128), 0) < 4
        tiles = []
        for m in range(8):
            at = 32 * m
            block = acc[c, at : at + 32, lanes] + grecv[at : at + 32, lanes].astype(F32)
            up, down = pltpu.roll(block[16:24], 4, 0), pltpu.roll(block[24:32], 4, 0)
            tiles += [block[:8], jnp.where(low, block[8:16], up), jnp.where(low, up, down)]
        mixed_grad = jnp.concatenate(tiles, axis=0)
        long_grad = mixed_grad * qf[:, lanes]
        query_grad = mixed_grad * ls[:, lanes]
        glb[:T, lanes] = long_grad
        gq[:, lanes] = query_grad
        head[:128, lanes] = long_grad[:128].astype(BF16)
        head[128:, lanes] = query_grad[:TAIL].astype(BF16)

    @pl.loop(0, 4)
    def _(l):
        gradients(l)

    head_copy = remote(head, head_in, h_s.at[3], h_r.at[3], prv)

    @pl.when(ctx > 0)
    def _():
        head_copy.start()

    @pl.loop(0, 4)
    def _(l):
        lanes = lane(l)
        grad = glb[:T, lanes]

        @pl.loop(0, 8)
        def _(r):
            for q in range(16):
                total[r, q : q + 1, lanes] = jnp.sum(
                    grad * rot[r, pl.ds(PRE - 8 * q, T), lanes], axis=0, keepdims=True
                )

        for t in range(8):
            part[l, t] = total[t, :, lanes].astype(BF16)

    def to_y(n):
        return remote(part.at[(y + n + 1) % NY], ybuf.at[n], py_s.at[n], py_r.at[n], ys[n])

    def taps_y(n):
        return remote(tpart.at[(y + n + 1) % NY], tybuf.at[n], ty_s.at[n], ty_r.at[n], ys[n])

    def to_z(n):
        return remote(mine.at[(zl + n + 1) % NZ], zbuf.at[n], pz_s.at[n], pz_r.at[n], zs_all[n])

    def taps_z(n):
        return remote(tmine, tzbuf.at[n], pt_s.at[n], pt_r.at[n], zs_all[n])

    def back_z(n):
        return remote(other.at[y, zl], other.at[y, zl], bz_s.at[n], bz_r.at[n], zs_all[n])

    def back_y(n):
        return remote(other.at[y], other.at[y], by_s.at[n], by_r.at[n], ys[n])

    for n in range(3):
        to_y(n).start()

    def finish(zs):
        collect(zs)
        out_far(zs).start()

    each(done, NZ, finish)

    @pl.when(ctx < last_ctx)
    def _():
        head_copy.wait_recv()

    @pl.loop(0, 4)
    def _(l):
        lanes = lane(l)
        glb[T:, lanes] = head_in[:128, lanes].astype(F32)
        full = glb[:, lanes]
        rg[0] = full
        for r in range(1, 8):
            rg[r] = pltpu.roll(full, full.shape[0] - r, 0)
        pair_grad = convolve(lambda r, at: rg[r, pl.ds(at, T)], 0, 1, lanes)
        key_grad = pair_grad * vf[:, lanes]
        value_grad = pair_grad * kf[:, lanes]
        gk[:, lanes] = key_grad
        gv[:, lanes] = value_grad
        lead[0, :, lanes] = key_grad[:TAIL].astype(BF16)
        lead[1, :, lanes] = value_grad[:TAIL].astype(BF16)
        for b, (at, grad) in enumerate(
            ((0, gq[:, lanes]), (PRE, key_grad), (2 * PRE, value_grad))
        ):
            raw = jnp.concatenate(
                [halo[at : at + TAIL, lanes].astype(F32), br_ref[b, :, lanes].astype(F32)], axis=0
            )
            for i in range(3):
                moved = raw if i == 0 else pltpu.roll(raw, i, 0)
                tg[3 * b + i : 3 * b + i + 1, lanes] = jnp.sum(grad * moved[TAIL:], axis=0, keepdims=True)
        tpart[l] = tg[:, lanes].astype(BF16)

    lead_copy = remote(lead, lead_in, h_s.at[4], h_r.at[4], prv)

    @pl.when(ctx > 0)
    def _():
        lead_copy.start()

    for n in range(3):
        taps_y(n).start()

    value = part[y].astype(F32)
    for n in range(3):
        to_y(n).wait_recv()
        value = value + ybuf[n].astype(F32)
    mine[...] = value.astype(BF16)
    for n in range(NZ - 1):
        to_z(n).start()

    @pl.when(ctx < last_ctx)
    def _():
        lead_copy.wait_recv()

    @pl.loop(0, 4)
    def _(l):
        lanes = lane(l)
        for b, (grad, ahead) in enumerate(
            ((gq, head_in[128:, lanes]), (gk, lead_in[0, :, lanes]), (gv, lead_in[1, :, lanes]))
        ):
            full = jnp.concatenate([grad[:, lanes], ahead.astype(F32)], axis=0)
            value = taps_ref[b, 0:1, lanes] * full
            for i in (1, 2):
                value = value + taps_ref[b, i : i + 1, lanes] * pltpu.roll(full, T + TAIL - i, 0)
            gin_ref[b, :, lanes] = value[:T].astype(BF16)

    value = tpart[y].astype(F32)
    for n in range(3):
        taps_y(n).wait_recv()
        value = value + tybuf[n].astype(F32)
    tmine[...] = value.astype(BF16)
    for n in range(NZ - 1):
        taps_z(n).start()
    value = mine[zl].astype(F32)
    for n in range(NZ - 1):
        to_z(n).wait_recv()
        value = value + zbuf[n].astype(F32)
    other[y, zl] = value.astype(BF16)
    for n in range(NZ - 1):
        back_z(n).start()

    for zs in range(NZ):
        out_far(zs).wait()
        for k in (0, 1):
            near[k, zs] = (sums[zh, zs, k].astype(F32) + far[zs, k].astype(F32)).astype(BF16)
    m_sib = remote(near.at[1 - c], come.at[c], sib_s.at[4], sib_r.at[4], sib)
    m_sib.start()

    value = tmine[...].astype(F32)
    for n in range(NZ - 1):
        taps_z(n).wait_recv()
        value = value + tzbuf[n].astype(F32)
    other[y, NZ] = value.astype(BF16)
    for n in range(NZ - 1):
        back_z(n).wait()
    for n in range(3):
        back_y(n).start()
    m_sib.wait()
    for k in (0, 1):
        for zs in range(NZ):
            for yy in range(NY):
                at = (zs * NY + yy) * 256
                lanes = slice(yy * 128, (yy + 1) * 128)

                @pl.when(c == k)
                def _(zs=zs, lanes=lanes, at=at, k=k):
                    mixed_ref[:, at + k * 128 : at + (k + 1) * 128] = near[k, zs, :, lanes][:12]

                @pl.when(c != k)
                def _(zs=zs, lanes=lanes, at=at, k=k):
                    mixed_ref[:, at + k * 128 : at + (k + 1) * 128] = come[k, zs, :, lanes][:12]

    for n in range(3):
        back_y(n).wait()
    for l in range(4):
        for t in range(8):
            total[t, :, l * 128 : (l + 1) * 128] = other[l, t].astype(F32)
        tg[:, l * 128 : (l + 1) * 128] = other[l, NZ].astype(F32)
    for j in range(128):
        gfil_ref[j : j + 1] = total[j % 8, j // 8 : j // 8 + 1]
    for b in range(3):
        gtap_ref[b] = tg[3 * b : 3 * b + 3]
    for n in range(3):
        to_y(n).wait_send()
        taps_y(n).wait_send()
    for n in range(NZ - 1):
        to_z(n).wait_send()
        taps_z(n).wait_send()

    @pl.when(ctx > 0)
    def _():
        head_copy.wait_send()
        lead_copy.wait_send()

    @pl.when(ctx < last_ctx)
    def _():
        for copy in halo_copies:
            copy.wait_send()

    @pl.loop(0, NZ)
    def _(zs):
        for h in (0, 1):
            y_plus(zs, y, h, 0).wait_send()
            y_minus(zs, y, h, 1).wait_send()
            y_plus(zs, y, h, 2).wait_send()

            @pl.when((zs <= zl) & (zl < NZ - 1))
            def _():
                z_right(zs, h).wait_send()

            @pl.when((zs >= zl) & (zl > 0))
            def _():
                z_left(zs, h).wait_send()

        for n in range(3):
            out_x(zs, n).wait_send()

    for k in (0, 1):
        cot_z(k).wait_send()
        for half in (0, 1):
            for n in range(3):
                cot_x(half, k, n).wait_send()


def block(branches, taps, filt, weight, cot):
    rows = weight.shape[0]
    wide = branches.shape[2]
    dma = pltpu.SemaphoreType.DMA
    vmem = pl.BlockSpec(memory_space=pltpu.VMEM)

    def f32(*shape):
        return pltpu.VMEM(shape, F32)

    def b16(*shape):
        return pltpu.VMEM(shape, BF16)

    return pl.pallas_call(
        block_kernel,
        out_shape=(
            jax.ShapeDtypeStruct((12, 8192), BF16),
            jax.ShapeDtypeStruct(branches.shape, BF16),
            jax.ShapeDtypeStruct(filt.shape, F32),
            jax.ShapeDtypeStruct(taps.shape, F32),
        ),
        in_specs=[vmem] * 5,
        out_specs=(vmem,) * 4,
        scratch_shapes=[
            f32(*taps.shape), f32(8, 16, wide),
            b16(NZ * NY, 2 * rows, 128), b16(4 * NX, 96, 512), b16(NZ, 256, 512), b16(TAIL + 2 * PRE, wide),
            f32(T, wide), f32(T, wide), f32(T, wide), f32(T, wide), f32(8, T + PRE, wide),
            b16(256, wide), b16(2, 256, wide), f32(2, 256, wide),
            b16(NZ, NX, 2, 32, 512), b16(NZ, 3, 2, 32, 512), b16(256, wide), b16(256, wide),
            b16(2, NZ, 2, 16, 512), b16(NZ, 2, 16, 512), b16(2, NZ, 16, 512), b16(2, NZ, 16, 512),
            b16(NY, NZ + 1, 16, 128),
            f32(T + 128, wide), f32(8, T + 128, 128), f32(T, wide), f32(T, wide), f32(T, wide),
            b16(128 + TAIL, wide), b16(128 + TAIL, wide), b16(2, TAIL, wide), b16(2, TAIL, wide), f32(16, wide),
            b16(NY, NZ, 16, 128), b16(NZ, 16, 128), b16(3, NZ, 16, 128), b16(NZ - 1, 16, 128), f32(8, 16, wide),
            b16(NY, 16, 128), b16(16, 128), b16(3, 16, 128), b16(NZ - 1, 16, 128),
            dma((3,)), dma((5,)), dma((5,)),
            dma((2, NZ, 2)), dma((NZ, 2)), dma((3, NZ, 2)), dma((3, NZ, 2)),
            dma((2, 2, 3)), dma((2, 2, 3)), dma((NZ, 3)), dma((NZ, 3)), dma((2,)), dma((2,)), dma((NZ,)), dma((NZ,)), dma((5,)), dma((5,)),
            dma((3,)), dma((3,)), dma((NZ - 1,)), dma((NZ - 1,)), dma((NZ - 1,)), dma((NZ - 1,)),
            dma((NZ - 1,)), dma((NZ - 1,)), dma((3,)), dma((3,)), dma((3,)), dma((3,)),
        ],
        compiler_params=pltpu.CompilerParams(
            collective_id=0, has_side_effects=True, vmem_limit_bytes=56 * 2**20
        ),
        name="hyena_block",
    )(branches, taps, filt, weight, cot)


def body(branch_inputs, feat_taps, long_filter, out_weight, cotangent):
    own_rows = cotangent.shape[0]
    cot_halves = (
        cotangent.reshape(own_rows, NZ, NY, 2, 128).transpose(3, 1, 0, 2, 4).reshape(2, NZ * own_rows, 512)
    )
    return block(branch_inputs, feat_taps, long_filter, out_weight, cot_halves)


def solution(mesh):
    placed = (
        P(None, "ctx", "tp"),
        P(None, None, "tp"),
        P(None, "tp"),
        P("tp", "ctx"),
        P(("ctx", "tp"), None),
    )
    return jax.shard_map(
        body,
        mesh=mesh,
        in_specs=placed,
        out_specs=(
            P(("ctx", "tp"), None),
            P(None, "ctx", "tp"),
            P(None, "tp"),
            P(None, None, "tp"),
        ),
        check_vma=False,
    )
```

```python
import functools

import jax
import jax.numpy as jnp
from jax import lax
from jax.experimental import pallas as pl
from jax.experimental.pallas import tpu as pltpu
from jax.sharding import PartitionSpec as P

MESH = pl.DeviceIdType.MESH
NZ, NY, NX = 8, 4, 4


def coords():
    ctx = lax.axis_index("ctx")
    tp = lax.axis_index("tp")
    return ctx, tp, ctx // NY, ctx % NY, tp // (2 * NX), (tp // 2) % NX, tp % 2


def device(zl, y, zh, x, c):
    return {"ctx": zl * NY + y, "tp": zh * (2 * NX) + x * 2 + c}


def remote(src, dst, send, recv, target):
    return pltpu.make_async_remote_copy(
        src_ref=src, dst_ref=dst, send_sem=send, recv_sem=recv, device_id=target, device_id_type=MESH
    )


def greet(targets):
    barrier = pltpu.get_barrier_semaphore()
    count = 0
    for target, there in targets:
        if there is True:
            pl.semaphore_signal(barrier, inc=1, device_id=target, device_id_type=MESH)
            count = count + 1
        else:
            @pl.when(there)
            def _():
                pl.semaphore_signal(barrier, inc=1, device_id=target, device_id_type=MESH)

            count = count + there.astype(jnp.int32)
    pl.semaphore_wait(barrier, count)


T = 192
PRE = 144
TAIL = 16
F32, BF16 = jnp.float32, jnp.bfloat16


def block_kernel(
    br_ref, ftaps_ref, filt_ref, w_ref, cot_ref,
    mixed_ref, gin_ref, gfil_ref, gtap_ref,
    taps_ref, fil_ref, wg, cp, cg, halo, qf, kf, vf, ls, rot, gated, both, acc, out, arrived, gsend, grecv,
    sums, far, near, come, other, glb, rg, gq, gk, gv, head, head_in, lead, lead_in, tg,
    part, mine, ybuf, zbuf, total, tpart, tmine, tybuf, tzbuf,
    own_sem, sib_s, sib_r, z_s, z_r, y_s, y_r, x_s, x_r, o_s, o_r, zp_s, zp_r, f_s, f_r, h_s, h_r,
    py_s, py_r, pz_s, pz_r, pt_s, pt_r, bz_s, bz_r, by_s, by_r, ty_s, ty_r,
):
    ctx, tp, zl, y, zh, x, c = coords()
    yp = device(zl, (y + 1) % NY, zh, x, c)
    ym = device(zl, (y + 3) % NY, zh, x, c)
    sib = device(zl, y, zh, x, 1 - c)
    zpart = device(zl, y, 1 - zh, x, c)
    xs = [device(zl, y, zh, (x + k) % NX, c) for k in (1, 2, 3)]
    ys = [device(zl, (y + k) % NY, zh, x, c) for k in (1, 2, 3)]
    zs_all = [device((zl + k) % NZ, y, zh, x, c) for k in range(1, NZ)]
    dright = device(jnp.minimum(zl + 1, NZ - 1), y, zh, x, c)
    dleft = device(jnp.maximum(zl - 1, 0), y, zh, x, c)
    last_ctx = NZ * NY - 1
    nxt = {"ctx": jnp.minimum(ctx + 1, last_ctx), "tp": tp}
    prv = {"ctx": jnp.maximum(ctx - 1, 0), "tp": tp}
    greet(
        [(sib, True), (zpart, True)]
        + [(d, True) for d in xs + ys + zs_all]
        + [(nxt, ctx < last_ctx), (prv, ctx > 0)]
    )
    rows = w_ref.shape[0]

    def unit(zs, yy, h):
        return wg.at[zs * NY + yy, pl.ds(pl.multiple_of(h * rows, rows), rows)]

    keep = w_ref.at[:, pl.ds(pl.multiple_of(c * 128, 128), 128)]
    give = w_ref.at[:, pl.ds(pl.multiple_of((1 - c) * 128, 128), 128)]
    w_sib = remote(give, unit(zl, y, c), sib_s.at[0], sib_r.at[0], sib)
    w_sib.start()
    w_own = pltpu.make_async_copy(keep, unit(zl, y, c), own_sem.at[0])
    w_own.start()
    c_sib = remote(cot_ref.at[1 - c], cp.at[tp], sib_s.at[1], sib_r.at[1], sib)
    c_sib.start()
    c_own = pltpu.make_async_copy(cot_ref.at[c], cp.at[tp], own_sem.at[1])
    c_own.start()
    halo_copies = [
        remote(br_ref.at[b, pl.ds(T - n, n)], halo.at[pl.ds(at, n)], h_s.at[b], h_r.at[b], nxt)
        for b, n, at in ((0, TAIL, 0), (1, PRE, TAIL), (2, PRE, TAIL + PRE))
    ]

    @pl.when(ctx < last_ctx)
    def _():
        for copy in halo_copies:
            copy.start()

    def z_right(zs, h):
        return remote(unit(zs, y, h), unit(zs, y, h), z_s.at[0, zs, h], z_r.at[zs, h], dright)

    def z_left(zs, h):
        return remote(unit(zs, y, h), unit(zs, y, h), z_s.at[1, zs, h], z_r.at[zs, h], dleft)

    def y_plus(zs, yy, h, kind):
        return remote(unit(zs, yy, h), unit(zs, yy, h), y_s.at[kind, zs, h], y_r.at[kind, zs, h], yp)

    def y_minus(zs, yy, h, kind):
        return remote(unit(zs, yy, h), unit(zs, yy, h), y_s.at[kind, zs, h], y_r.at[kind, zs, h], ym)

    def spread(zs, h):
        y_plus(zs, y, h, 0).start()
        y_minus(zs, y, h, 1).start()

    def relay(zs, h):
        y_plus(zs, (y + 3) % NY, h, 0).wait_recv()
        y_minus(zs, (y + 1) % NY, h, 1).wait_recv()

        upward = (h == 0) & (zs != zl)

        @pl.when(upward)
        def _():
            y_plus(zs, (y + 3) % NY, h, 2).start()

        @pl.when(jnp.logical_not(upward))
        def _():
            y_minus(zs, (y + 1) % NY, h, 2).start()

    def cot_z(k):
        piece = zh * (2 * NX) + x * 2 + k
        return remote(cp.at[piece], cp.at[piece], zp_s.at[k], zp_r.at[k], zpart)

    def cot_x(half, k, n):
        piece = half * (2 * NX) + x * 2 + k
        return remote(cp.at[piece], cp.at[piece], x_s.at[half, k, n], x_r.at[half, k, n], xs[n])

    def out_x(zs, n):
        return remote(out.at[zs, (x + n + 1) % NX], arrived.at[zs, n], o_s.at[zs, n], o_r.at[zs, n], xs[n])

    order = (c, 1 - c)
    w_own.wait()
    for h in order:
        if h is not c:
            w_sib.wait()

        @pl.when(zl < NZ - 1)
        def _(h=h):
            z_right(zl, h).start()

        @pl.when(zl > 0)
        def _(h=h):
            z_left(zl, h).start()

        spread(zl, h)
        if h is c:
            c_own.wait()
        else:
            c_sib.wait()
        cot_z(h).start()
        for n in range(3):
            cot_x(zh, h, n).start()
    for b in range(3):
        taps_ref[b] = ftaps_ref[b].astype(F32)
    for j in range(128):
        fil_ref[j % 8, j // 8 : j // 8 + 1] = filt_ref[j : j + 1]
    acc[...] = jnp.zeros_like(acc)
    tg[...] = jnp.zeros_like(tg)

    @pl.when(ctx == 0)
    def _():
        halo[...] = jnp.zeros_like(halo)

    @pl.when(ctx == last_ctx)
    def _():
        head_in[...] = jnp.zeros_like(head_in)
        lead_in[...] = jnp.zeros_like(lead_in)

    def lane(l):
        return pl.ds(pl.multiple_of(l * 128, 128), 128)

    def spaced(value, count):
        shifted = pltpu.roll(value, value.shape[0] - 4, 0)
        for i in range(count):
            at = 12 * i
            yield (value[at : at + 16] if at % 8 == 0 else shifted[at - 4 : at + 12]).astype(BF16)

    def dense(value):
        low = lax.broadcasted_iota(jnp.int32, (8, value.shape[1]), 0) < 4
        up, down = pltpu.roll(value[16:24], 4, 0), pltpu.roll(value[24:32], 4, 0)
        return [value[:8], jnp.where(low, value[8:16], up), jnp.where(low, up, down)]

    def convolve(source, first, step, lanes):
        def residue(r, value):
            for q in range(16):
                tap = fil_ref[r, q : q + 1, lanes]
                value = value + tap * source(r, first + step * 8 * q)
            return value

        return lax.fori_loop(0, 8, residue, jnp.zeros((T, 128), F32))

    def features(l):
        lanes = lane(l)

        def feature(b, at, n):
            raw = jnp.concatenate([halo[at : at + n, lanes].astype(F32), br_ref[b, :, lanes].astype(F32)], axis=0)
            value = taps_ref[b, 0:1, lanes] * raw
            for i in (1, 2):
                value = value + taps_ref[b, i : i + 1, lanes] * pltpu.roll(raw, i, 0)
            return value.astype(BF16).astype(F32)

        query = feature(0, 0, TAIL)[TAIL:]
        key = feature(1, TAIL, PRE)
        value = feature(2, TAIL + PRE, PRE)
        qf[:, lanes] = query
        kf[:, lanes] = key[PRE:]
        vf[:, lanes] = value[PRE:]
        pair = (key * value).astype(BF16).astype(F32)
        rot[0, :, lanes] = pair
        for r in range(1, 8):
            rot[r, :, lanes] = pltpu.roll(pair, r, 0)
        long = convolve(lambda r, at: rot[r, pl.ds(at, T), lanes], PRE, -1, lanes)
        ls[:, lanes] = long
        for i, rows16 in enumerate(spaced(query * long, 16)):
            gated[16 * i : 16 * i + 16, lanes] = rows16

    def weight(zs, k):
        return jnp.concatenate([wg[zs * NY + yy, k * rows : (k + 1) * rows] for yy in range(NY)], axis=1)

    def forward(zs):
        value = jnp.dot(both[0], weight(zs, 0), preferred_element_type=F32)
        value = value + jnp.dot(both[1], weight(zs, 1), preferred_element_type=F32)
        for xx in range(NX):
            groups = []
            for half in (0, 1):
                at = (half * NX + xx) * 32
                groups += dense(value[at : at + 32])
            out[zs, xx] = jnp.concatenate(groups, axis=0).astype(BF16)
        for n in range(3):
            out_x(zs, n).start()

    def backward(zs):
        for k in (0, 1):
            acc[k] += lax.dot_general(
                cg[zs], weight(zs, k), (((1,), (1,)), ((), ())), preferred_element_type=F32
            )

    def collect(zs):
        value = out[zs, x].astype(F32)
        for n in range(3):
            out_x(zs, n).wait_recv()
            value = value + arrived[zs, n].astype(F32)
        for half in (0, 1):
            own = value[24 * half : 24 * half + 24]
            sums[half, zs] = jnp.concatenate([own[:, :256], own[:, 256:]], axis=0).astype(BF16)

    def out_far(zs):
        return remote(sums.at[1 - zh, zs], far.at[zs], f_s.at[zs], f_r.at[zs], zpart)

    near_end = jnp.minimum(zl, NZ - 1 - zl)

    def nth(n):
        paired = jnp.where(n % 2 == 1, zl - (n + 1) // 2, zl + n // 2)
        single = jnp.where(zl < NZ // 2, zl + (n - near_end), zl - (n - near_end))
        return jnp.where(n <= 2 * near_end, paired, single)

    def each(first, last, act):
        @pl.loop(first, last)
        def _(n):
            act(nth(n))

    x_sib = remote(gated, both.at[c], sib_s.at[2], sib_r.at[2], sib)
    x_own = pltpu.make_async_copy(gated, both.at[c], own_sem.at[2])

    def forward_done(step):
        return jnp.maximum(0, jnp.minimum(2 * (step - 2), step - 1))

    def backward_done(step):
        return jnp.maximum(0, jnp.minimum(3 * (step - 5), step - 1))

    @pl.loop(1, NZ + 2)
    def _(step):
        for h in order:
            @pl.when((zl - step >= 0) & (step < NZ))
            def _(h=h):
                z_right(zl - step, h).wait_recv()

                @pl.when(zl < NZ - 1)
                def _():
                    z_right(zl - step, h).start()

            @pl.when(zl + step < NZ)
            def _(h=h):
                z_left(zl + step, h).wait_recv()

                @pl.when(zl > 0)
                def _():
                    z_left(zl + step, h).start()

        def pass_on(zs):
            for h in order:
                relay(zs, h)

        def relayed(zs):
            for h in (0, 1):
                y_plus(zs, (y + 2) % NY, h, 2).wait_recv()

        @pl.when(step < NZ)
        def _():
            for h in order:
                spread(nth(step), h)

        @pl.when(step <= NZ)
        def _():
            pass_on(nth(step - 1))

        @pl.when(step >= 2)
        def _():
            relayed(nth(step - 2))

        @pl.when((step == 1) & (ctx > 0))
        def _():
            for copy in halo_copies:
                copy.wait_recv()

        @pl.when(step <= 2)
        def _():
            @pl.loop(2 * step - 2, 2 * step)
            def _(l):
                features(l)

        @pl.when(step == 2)
        def _():
            x_sib.start()
            x_own.start()

        @pl.when(step == 4)
        def _():
            for k in order:
                cot_z(k).wait_recv()
                for n in range(3):
                    cot_x(1 - zh, k, n).start()

        @pl.when(step == 3)
        def _():
            x_own.wait()
            x_sib.wait()

        @pl.when(step == 6)
        def _():
            for k in (0, 1):
                for half in (0, 1):
                    for n in range(3):
                        cot_x(half, k, n).wait_recv()

            @pl.loop(0, 4 * NX)
            def _(piece):
                at = pl.ds(pl.multiple_of(piece * 16, 16), 16)
                for zs, rows16 in enumerate(spaced(cp[piece].astype(F32), NZ)):
                    cg[zs, at] = rows16

        each(forward_done(step - 1), forward_done(step), forward)
        each(backward_done(step - 1), backward_done(step), backward)
        each(forward_done(step - 3), forward_done(step - 2), collect)

        @pl.when(step >= NZ - 1)
        def _():
            each(jnp.where(step == NZ - 1, 0, forward_done(step - 3)), forward_done(step - 2), lambda zs: out_far(zs).start())

    gsend[...] = acc[1 - c].astype(BF16)
    g_sib = remote(gsend, grecv, sib_s.at[3], sib_r.at[3], sib)
    g_sib.start()

    g_sib.wait()

    def gradients(l):
        lanes = lane(l)
        tiles = []
        for m in range(8):
            at = 32 * m
            block = acc[c, at : at + 32, lanes] + grecv[at : at + 32, lanes].astype(F32)
            tiles += dense(block)
        mixed_grad = jnp.concatenate(tiles, axis=0)
        long_grad = mixed_grad * qf[:, lanes]
        query_grad = mixed_grad * ls[:, lanes]
        glb[:T, lanes] = long_grad
        gq[:, lanes] = query_grad
        head[:128, lanes] = long_grad[:128].astype(BF16)
        head[128:, lanes] = query_grad[:TAIL].astype(BF16)

    @pl.loop(0, 4)
    def _(l):
        gradients(l)

    head_copy = remote(head, head_in, h_s.at[3], h_r.at[3], prv)

    @pl.when(ctx > 0)
    def _():
        head_copy.start()

    @pl.loop(0, 4)
    def _(l):
        lanes = lane(l)
        grad = glb[:T, lanes]

        @pl.loop(0, 8)
        def _(r):
            for q in range(16):
                total[r, q : q + 1, lanes] = jnp.sum(
                    grad * rot[r, pl.ds(PRE - 8 * q, T), lanes], axis=0, keepdims=True
                )

        for t in range(8):
            part[l, t] = total[t, :, lanes].astype(BF16)

    def to_y(n):
        return remote(part.at[(y + n + 1) % NY], ybuf.at[n], py_s.at[n], py_r.at[n], ys[n])

    def taps_y(n):
        return remote(tpart.at[(y + n + 1) % NY], tybuf.at[n], ty_s.at[n], ty_r.at[n], ys[n])

    def to_z(n):
        return remote(mine.at[(zl + n + 1) % NZ], zbuf.at[n], pz_s.at[n], pz_r.at[n], zs_all[n])

    def taps_z(n):
        return remote(tmine, tzbuf.at[n], pt_s.at[n], pt_r.at[n], zs_all[n])

    def back_z(n):
        return remote(other.at[y, zl], other.at[y, zl], bz_s.at[n], bz_r.at[n], zs_all[n])

    def back_y(n):
        return remote(other.at[y], other.at[y], by_s.at[n], by_r.at[n], ys[n])

    for n in range(3):
        to_y(n).start()

    def finish(zs):
        collect(zs)
        out_far(zs).start()

    each(forward_done(NZ - 1), NZ, finish)

    @pl.when(ctx < last_ctx)
    def _():
        head_copy.wait_recv()

    @pl.loop(0, 4)
    def _(l):
        lanes = lane(l)
        glb[T:, lanes] = head_in[:128, lanes].astype(F32)
        full = glb[:, lanes]
        rg[0] = full
        for r in range(1, 8):
            rg[r] = pltpu.roll(full, full.shape[0] - r, 0)
        pair_grad = convolve(lambda r, at: rg[r, pl.ds(at, T)], 0, 1, lanes)
        key_grad = pair_grad * vf[:, lanes]
        value_grad = pair_grad * kf[:, lanes]
        gk[:, lanes] = key_grad
        gv[:, lanes] = value_grad
        lead[0, :, lanes] = key_grad[:TAIL].astype(BF16)
        lead[1, :, lanes] = value_grad[:TAIL].astype(BF16)
        for b, (at, grad) in enumerate(
            ((0, gq[:, lanes]), (PRE, key_grad), (2 * PRE, value_grad))
        ):
            raw = jnp.concatenate(
                [halo[at : at + TAIL, lanes].astype(F32), br_ref[b, :, lanes].astype(F32)], axis=0
            )
            for i in range(3):
                moved = raw if i == 0 else pltpu.roll(raw, i, 0)
                tg[3 * b + i : 3 * b + i + 1, lanes] = jnp.sum(grad * moved[TAIL:], axis=0, keepdims=True)
        tpart[l] = tg[:, lanes].astype(BF16)

    lead_copy = remote(lead, lead_in, h_s.at[4], h_r.at[4], prv)

    @pl.when(ctx > 0)
    def _():
        lead_copy.start()

    for n in range(3):
        taps_y(n).start()

    value = part[y].astype(F32)
    for n in range(3):
        to_y(n).wait_recv()
        value = value + ybuf[n].astype(F32)
    mine[...] = value.astype(BF16)
    for n in range(NZ - 1):
        to_z(n).start()

    value = tpart[y].astype(F32)
    for n in range(3):
        taps_y(n).wait_recv()
        value = value + tybuf[n].astype(F32)
    tmine[...] = value.astype(BF16)
    for n in range(NZ - 1):
        taps_z(n).start()

    @pl.when(ctx < last_ctx)
    def _():
        lead_copy.wait_recv()

    @pl.loop(0, 4)
    def _(l):
        lanes = lane(l)
        for b, (grad, ahead) in enumerate(
            ((gq, head_in[128:, lanes]), (gk, lead_in[0, :, lanes]), (gv, lead_in[1, :, lanes]))
        ):
            full = jnp.concatenate([grad[:, lanes], ahead.astype(F32)], axis=0)
            value = taps_ref[b, 0:1, lanes] * full
            for i in (1, 2):
                value = value + taps_ref[b, i : i + 1, lanes] * pltpu.roll(full, T + TAIL - i, 0)
            gin_ref[b, :, lanes] = value[:T].astype(BF16)

    value = mine[zl].astype(F32)
    for n in range(NZ - 1):
        to_z(n).wait_recv()
        value = value + zbuf[n].astype(F32)
    other[y, zl] = value.astype(BF16)
    for n in range(NZ - 1):
        back_z(n).start()

    for zs in range(NZ):
        out_far(zs).wait()
        value = sums[zh, zs].astype(F32) + far[zs].astype(F32)
        value = jnp.concatenate([value[:24], value[24:]], axis=1)
        for k, rows16 in enumerate(spaced(value, 2)):
            near[k, zs] = rows16
    m_sib = remote(near.at[1 - c], come.at[c], sib_s.at[4], sib_r.at[4], sib)
    m_sib.start()

    value = tmine[...].astype(F32)
    for n in range(NZ - 1):
        taps_z(n).wait_recv()
        value = value + tzbuf[n].astype(F32)
    other[y, NZ] = value.astype(BF16)
    for n in range(NZ - 1):
        back_z(n).wait()
    for n in range(3):
        back_y(n).start()
    m_sib.wait()
    for k in (0, 1):
        for zs in range(NZ):
            for yy in range(NY):
                at = (zs * NY + yy) * 256
                lanes = slice(yy * 128, (yy + 1) * 128)

                @pl.when(c == k)
                def _(zs=zs, lanes=lanes, at=at, k=k):
                    mixed_ref[:, at + k * 128 : at + (k + 1) * 128] = near[k, zs, :, lanes][:12]

                @pl.when(c != k)
                def _(zs=zs, lanes=lanes, at=at, k=k):
                    mixed_ref[:, at + k * 128 : at + (k + 1) * 128] = come[k, zs, :, lanes][:12]

    for n in range(3):
        back_y(n).wait()
    for l in range(4):
        for t in range(8):
            total[t, :, l * 128 : (l + 1) * 128] = other[l, t].astype(F32)
        tg[:, l * 128 : (l + 1) * 128] = other[l, NZ].astype(F32)
    for j in range(128):
        gfil_ref[j : j + 1] = total[j % 8, j // 8 : j // 8 + 1]
    for b in range(3):
        gtap_ref[b] = tg[3 * b : 3 * b + 3]
    for n in range(3):
        to_y(n).wait_send()
        taps_y(n).wait_send()
    for n in range(NZ - 1):
        to_z(n).wait_send()
        taps_z(n).wait_send()

    @pl.when(ctx > 0)
    def _():
        head_copy.wait_send()
        lead_copy.wait_send()

    @pl.when(ctx < last_ctx)
    def _():
        for copy in halo_copies:
            copy.wait_send()

    @pl.loop(0, NZ)
    def _(zs):
        for h in (0, 1):
            y_plus(zs, y, h, 0).wait_send()
            y_minus(zs, y, h, 1).wait_send()
            y_plus(zs, y, h, 2).wait_send()

            @pl.when((zs <= zl) & (zl < NZ - 1))
            def _():
                z_right(zs, h).wait_send()

            @pl.when((zs >= zl) & (zl > 0))
            def _():
                z_left(zs, h).wait_send()

        for n in range(3):
            out_x(zs, n).wait_send()

    for k in (0, 1):
        cot_z(k).wait_send()
        for half in (0, 1):
            for n in range(3):
                cot_x(half, k, n).wait_send()


def block(branches, taps, filt, weight, cot):
    rows = weight.shape[0]
    wide = branches.shape[2]
    dma = pltpu.SemaphoreType.DMA
    vmem = pl.BlockSpec(memory_space=pltpu.VMEM)

    def f32(*shape):
        return pltpu.VMEM(shape, F32)

    def b16(*shape):
        return pltpu.VMEM(shape, BF16)

    return pl.pallas_call(
        block_kernel,
        out_shape=(
            jax.ShapeDtypeStruct((12, 8192), BF16),
            jax.ShapeDtypeStruct(branches.shape, BF16),
            jax.ShapeDtypeStruct(filt.shape, F32),
            jax.ShapeDtypeStruct(taps.shape, F32),
        ),
        in_specs=[vmem] * 5,
        out_specs=(vmem,) * 4,
        scratch_shapes=[
            f32(*taps.shape), f32(8, 16, wide),
            b16(NZ * NY, 2 * rows, 128), b16(4 * NX, 96, 512), b16(NZ, 256, 512), b16(TAIL + 2 * PRE, wide),
            f32(T, wide), f32(T, wide), f32(T, wide), f32(T, wide), f32(8, T + PRE, wide),
            b16(256, wide), b16(2, 256, wide), f32(2, 256, wide),
            b16(NZ, NX, 48, 512), b16(NZ, 3, 48, 512), b16(256, wide), b16(256, wide),
            b16(2, NZ, 48, 256), b16(NZ, 48, 256), b16(2, NZ, 16, 512), b16(2, NZ, 16, 512),
            b16(NY, NZ + 1, 16, 128),
            f32(T + 128, wide), f32(8, T + 128, 128), f32(T, wide), f32(T, wide), f32(T, wide),
            b16(128 + TAIL, wide), b16(128 + TAIL, wide), b16(2, TAIL, wide), b16(2, TAIL, wide), f32(16, wide),
            b16(NY, NZ, 16, 128), b16(NZ, 16, 128), b16(3, NZ, 16, 128), b16(NZ - 1, 16, 128), f32(8, 16, wide),
            b16(NY, 16, 128), b16(16, 128), b16(3, 16, 128), b16(NZ - 1, 16, 128),
            dma((3,)), dma((5,)), dma((5,)),
            dma((2, NZ, 2)), dma((NZ, 2)), dma((3, NZ, 2)), dma((3, NZ, 2)),
            dma((2, 2, 3)), dma((2, 2, 3)), dma((NZ, 3)), dma((NZ, 3)), dma((2,)), dma((2,)), dma((NZ,)), dma((NZ,)), dma((5,)), dma((5,)),
            dma((3,)), dma((3,)), dma((NZ - 1,)), dma((NZ - 1,)), dma((NZ - 1,)), dma((NZ - 1,)),
            dma((NZ - 1,)), dma((NZ - 1,)), dma((3,)), dma((3,)), dma((3,)), dma((3,)),
        ],
        compiler_params=pltpu.CompilerParams(
            collective_id=0, has_side_effects=True, vmem_limit_bytes=56 * 2**20
        ),
        name="hyena_block",
    )(branches, taps, filt, weight, cot)


def body(branch_inputs, feat_taps, long_filter, out_weight, cotangent):
    own_rows = cotangent.shape[0]
    cot_halves = (
        cotangent.reshape(own_rows, NZ, NY, 2, 128).transpose(3, 1, 0, 2, 4).reshape(2, NZ * own_rows, 512)
    )
    return block(branch_inputs, feat_taps, long_filter, out_weight, cot_halves)


def solution(mesh):
    placed = (
        P(None, "ctx", "tp"),
        P(None, None, "tp"),
        P(None, "tp"),
        P("tp", "ctx"),
        P(("ctx", "tp"), None),
    )
    return jax.shard_map(
        body,
        mesh=mesh,
        in_specs=placed,
        out_specs=(
            P(("ctx", "tp"), None),
            P(None, "ctx", "tp"),
            P(None, "tp"),
            P(None, None, "tp"),
        ),
        check_vma=False,
    )
```

```python
import functools

import jax
import jax.numpy as jnp
from jax import lax
from jax.experimental import pallas as pl
from jax.experimental.pallas import tpu as pltpu
from jax.sharding import PartitionSpec as P

MESH = pl.DeviceIdType.MESH
NZ, NY, NX = 8, 4, 4


def coords():
    ctx = lax.axis_index("ctx")
    tp = lax.axis_index("tp")
    return ctx, tp, ctx // NY, ctx % NY, tp // (2 * NX), (tp // 2) % NX, tp % 2


def device(zl, y, zh, x, c):
    return {"ctx": zl * NY + y, "tp": zh * (2 * NX) + x * 2 + c}


def remote(src, dst, send, recv, target):
    return pltpu.make_async_remote_copy(
        src_ref=src, dst_ref=dst, send_sem=send, recv_sem=recv, device_id=target, device_id_type=MESH
    )


def greet(targets):
    barrier = pltpu.get_barrier_semaphore()
    count = 0
    for target, there in targets:
        if there is True:
            pl.semaphore_signal(barrier, inc=1, device_id=target, device_id_type=MESH)
            count = count + 1
        else:
            @pl.when(there)
            def _():
                pl.semaphore_signal(barrier, inc=1, device_id=target, device_id_type=MESH)

            count = count + there.astype(jnp.int32)
    pl.semaphore_wait(barrier, count)


T = 192
PRE = 144
TAIL = 16
F32, BF16 = jnp.float32, jnp.bfloat16


def block_kernel(
    br_ref, ftaps_ref, filt_ref, w_ref, cot_in,
    mixed_ref, gin_ref, gfil_ref, gtap_ref,
    cot16, cot_ref, taps_ref, fil_ref, wg, cp, cg, halo, qf, kf, vf, ls, rot, gated, both, acc, out, arrived, gsend, grecv,
    sums, far, near, come, other, glb, rg, gq, gk, gv, head, head_in, lead, lead_in, tg,
    part, mine, ybuf, zbuf, total, tpart, tmine, tybuf, tzbuf,
    own_sem, sib_s, sib_r, cy_s, cy_r, xp_s, xp_r, g_s, g_r, m_s, m_r, z_s, z_r, y_s, y_r, x_s, x_r, o_s, o_r, zp_s, zp_r, f_s, f_r, h_s, h_r,
    py_s, py_r, pz_s, pz_r, pt_s, pt_r, bz_s, bz_r, by_s, by_r, ty_s, ty_r,
):
    ctx, tp, zl, y, zh, x, c = coords()
    t = y % 2
    yx, ps, js = y + 1 - 2 * t, ((y + 1) // 2) % 2, y // 2
    wy = device(zl, 3 - y, zh, x, c)
    part_same, part_other = device(zl, yx, zh, x, c), device(zl, yx, zh, x, 1 - c)
    sib = device(zl, y, zh, x, 1 - c)
    zpart = device(zl, y, 1 - zh, x, c)
    xs = [device(zl, y, zh, (x + k) % NX, c) for k in (1, 2, 3)]
    ys = [device(zl, (y + k) % NY, zh, x, c) for k in (1, 2, 3)]
    zs_all = [device((zl + k) % NZ, y, zh, x, c) for k in range(1, NZ)]
    dright = device(jnp.minimum(zl + 1, NZ - 1), y, zh, x, c)
    dleft = device(jnp.maximum(zl - 1, 0), y, zh, x, c)
    last_ctx = NZ * NY - 1
    nxt = {"ctx": jnp.minimum(ctx + 1, last_ctx), "tp": tp}
    prv = {"ctx": jnp.maximum(ctx - 1, 0), "tp": tp}
    greet(
        [(sib, True), (zpart, True), (part_other, True)]
        + [(d, True) for d in xs + ys + zs_all]
        + [(nxt, ctx < last_ctx), (prv, ctx > 0)]
    )
    rows = w_ref.shape[0]

    def unit(zs, j, h):
        return wg.at[zs * 2 + j, pl.ds(pl.multiple_of(h * rows, rows), rows)]

    def token_rows(which):
        return pl.ds(pl.multiple_of(which * 256, 256), 256)

    def cot_rows(which):
        return pl.ds(pl.multiple_of(which * 96, 96), 96)

    keep = w_ref.at[:, pl.ds(pl.multiple_of(c * 128, 128), 128)]
    give = w_ref.at[:, pl.ds(pl.multiple_of((1 - c) * 128, 128), 128)]
    w_sib = remote(give, unit(zl, js, c), sib_s.at[0], sib_r.at[0], sib)
    w_sib.start()
    w_own = pltpu.make_async_copy(keep, unit(zl, js, c), own_sem.at[0])
    w_own.start()
    halo_copies = [
        remote(br_ref.at[b, pl.ds(T - n, n)], halo.at[pl.ds(at, n)], h_s.at[b], h_r.at[b], nxt)
        for b, n, at in ((0, TAIL, 0), (1, PRE, TAIL), (2, PRE, TAIL + PRE))
    ]

    @pl.when(ctx < last_ctx)
    def _():
        for copy in halo_copies:
            copy.start()

    def dense(value):
        low = lax.broadcasted_iota(jnp.int32, (8, value.shape[1]), 0) < 4
        up, down = pltpu.roll(value[16:24], 4, 0), pltpu.roll(value[24:32], 4, 0)
        return [value[:8], jnp.where(low, value[8:16], up), jnp.where(low, up, down)]

    cot16[...] = jnp.zeros_like(cot16)
    cot16[:12] = cot_in[...]
    for p, both_y in enumerate(((0, 3), (1, 2))):
        for k in (0, 1):
            for j, yy in enumerate(both_y):
                tiles = []
                for m in range(NZ // 2):
                    pair = [
                        cot16[:, pl.ds(((2 * m + n) * NY + yy) * 256 + k * 128, 128)].astype(F32) for n in (0, 1)
                    ]
                    tiles += dense(jnp.concatenate(pair, axis=0))
                cot_ref[p, k, :, j * 128 : (j + 1) * 128] = jnp.concatenate(tiles, axis=0).astype(BF16)
    c_here = cp.at[tp, cot_rows(t)]
    c_sib = remote(cot_ref.at[ps, 1 - c], c_here, sib_s.at[1], sib_r.at[1], sib)
    c_pair = [
        remote(cot_ref.at[1 - ps, c], c_here, cy_s.at[0], cy_r.at[0], part_same),
        remote(cot_ref.at[1 - ps, 1 - c], c_here, cy_s.at[1], cy_r.at[1], part_other),
    ]
    c_own = pltpu.make_async_copy(cot_ref.at[ps, c], c_here, own_sem.at[1])
    for copy in [c_sib, c_own] + c_pair:
        copy.start()
    def z_right(zs, h):
        return remote(unit(zs, js, h), unit(zs, js, h), z_s.at[0, zs, h], z_r.at[zs, h], dright)

    def z_left(zs, h):
        return remote(unit(zs, js, h), unit(zs, js, h), z_s.at[1, zs, h], z_r.at[zs, h], dleft)

    def across(zs, j, h):
        return remote(unit(zs, j, h), unit(zs, j, h), y_s.at[zs, h], y_r.at[zs, h], wy)

    def spread(zs, h):
        across(zs, js, h).start()

    def cot_z(k):
        piece = zh * (2 * NX) + x * 2 + k
        return remote(cp.at[piece], cp.at[piece], zp_s.at[k], zp_r.at[k], zpart)

    def cot_x(half, k, n):
        piece = half * (2 * NX) + x * 2 + k
        return remote(cp.at[piece], cp.at[piece], x_s.at[half, k, n], x_r.at[half, k, n], xs[n])

    def out_x(zs, n):
        return remote(out.at[zs, (x + n + 1) % NX], arrived.at[zs, n], o_s.at[zs, n], o_r.at[zs, n], xs[n])

    order = (c, 1 - c)
    w_own.wait()
    for h in order:
        if h is not c:
            w_sib.wait()

        @pl.when(zl < NZ - 1)
        def _(h=h):
            z_right(zl, h).start()

        @pl.when(zl > 0)
        def _(h=h):
            z_left(zl, h).start()

        spread(zl, h)
        if h is c:
            c_own.wait()
            c_pair[0].wait_recv()
        else:
            c_sib.wait()
            c_pair[1].wait_recv()
        cot_z(h).start()
        for n in range(3):
            cot_x(zh, h, n).start()
    for b in range(3):
        taps_ref[b] = ftaps_ref[b].astype(F32)
    for j in range(128):
        fil_ref[j % 8, j // 8 : j // 8 + 1] = filt_ref[j : j + 1]
    acc[...] = jnp.zeros_like(acc)
    tg[...] = jnp.zeros_like(tg)

    @pl.when(ctx == 0)
    def _():
        halo[...] = jnp.zeros_like(halo)

    @pl.when(ctx == last_ctx)
    def _():
        head_in[...] = jnp.zeros_like(head_in)
        lead_in[...] = jnp.zeros_like(lead_in)

    def lane(l):
        return pl.ds(pl.multiple_of(l * 128, 128), 128)

    def spaced(value, count):
        shifted = pltpu.roll(value, value.shape[0] - 4, 0)
        for i in range(count):
            at = 12 * i
            yield (value[at : at + 16] if at % 8 == 0 else shifted[at - 4 : at + 12]).astype(BF16)

    def convolve(source, first, step, lanes):
        def residue(r, value):
            for q in range(16):
                tap = fil_ref[r, q : q + 1, lanes]
                value = value + tap * source(r, first + step * 8 * q)
            return value

        return lax.fori_loop(0, 8, residue, jnp.zeros((T, 128), F32))

    def features(l):
        lanes = lane(l)

        def feature(b, at, n):
            raw = jnp.concatenate([halo[at : at + n, lanes].astype(F32), br_ref[b, :, lanes].astype(F32)], axis=0)
            value = taps_ref[b, 0:1, lanes] * raw
            for i in (1, 2):
                value = value + taps_ref[b, i : i + 1, lanes] * pltpu.roll(raw, i, 0)
            return value.astype(BF16).astype(F32)

        query = feature(0, 0, TAIL)[TAIL:]
        key = feature(1, TAIL, PRE)
        value = feature(2, TAIL + PRE, PRE)
        qf[:, lanes] = query
        kf[:, lanes] = key[PRE:]
        vf[:, lanes] = value[PRE:]
        pair = (key * value).astype(BF16).astype(F32)
        rot[0, :, lanes] = pair
        for r in range(1, 8):
            rot[r, :, lanes] = pltpu.roll(pair, r, 0)
        long = convolve(lambda r, at: rot[r, pl.ds(at, T), lanes], PRE, -1, lanes)
        ls[:, lanes] = long
        for i, rows16 in enumerate(spaced(query * long, 16)):
            gated[16 * i : 16 * i + 16, lanes] = rows16

    def weight(zs, k):
        return jnp.concatenate([wg[zs * 2 + j, k * rows : (k + 1) * rows] for j in (0, 1)], axis=1)

    def forward(zs):
        value = jnp.dot(both[0], weight(zs, 0), preferred_element_type=F32)
        value = value + jnp.dot(both[1], weight(zs, 1), preferred_element_type=F32)
        for xx in range(NX):
            groups = []
            for which in (0, 1):
                for half in (0, 1):
                    at = which * 256 + (half * NX + xx) * 32
                    groups += dense(value[at : at + 32])
            out[zs, xx] = jnp.concatenate(groups, axis=0).astype(BF16)
        for n in range(3):
            out_x(zs, n).start()

    def backward(zs):
        for k in (0, 1):
            acc[k] += lax.dot_general(
                cg[zs], weight(zs, k), (((1,), (1,)), ((), ())), preferred_element_type=F32
            )

    def collect(zs):
        value = out[zs, x].astype(F32)
        for n in range(3):
            out_x(zs, n).wait_recv()
            value = value + arrived[zs, n].astype(F32)
        for half in (0, 1):
            at = 24 * half
            sums[half, zs] = jnp.concatenate([value[at : at + 24], value[48 + at : 72 + at]], axis=0).astype(BF16)

    def out_far(zs):
        return remote(sums.at[1 - zh, zs], far.at[zs], f_s.at[zs], f_r.at[zs], zpart)

    near_end = jnp.minimum(zl, NZ - 1 - zl)

    def nth(n):
        paired = jnp.where(n % 2 == 1, zl - (n + 1) // 2, zl + n // 2)
        single = jnp.where(zl < NZ // 2, zl + (n - near_end), zl - (n - near_end))
        return jnp.where(n <= 2 * near_end, paired, single)

    def each(first, last, act):
        @pl.loop(first, last)
        def _(n):
            act(nth(n))

    x_here = both.at[c, token_rows(t)]
    x_out = [
        remote(gated, x_here, xp_s.at[n], xp_r.at[n], to) for n, to in enumerate((sib, part_same, part_other))
    ]
    x_own = pltpu.make_async_copy(gated, x_here, own_sem.at[2])

    def forward_done(step):
        return jnp.maximum(0, jnp.minimum(2 * (step - 2), step))

    def backward_done(step):
        return jnp.maximum(0, jnp.minimum(3 * (step - 5), step))

    @pl.loop(1, NZ + 1)
    def _(step):
        def pass_on(h):
            @pl.when(zl - step >= 0)
            def _():
                z_right(zl - step, h).wait_recv()

                @pl.when(zl < NZ - 1)
                def _():
                    z_right(zl - step, h).start()

            @pl.when(zl + step < NZ)
            def _():
                z_left(zl + step, h).wait_recv()

                @pl.when(zl > 0)
                def _():
                    z_left(zl + step, h).start()

            @pl.when(step < NZ)
            def _():
                spread(nth(step), h)

        pass_on(c)
        for h in order:
            across(nth(step - 1), 1 - js, h).wait_recv()

        @pl.when((step == 1) & (ctx > 0))
        def _():
            for copy in halo_copies:
                copy.wait_recv()

        @pl.when(step <= 2)
        def _():
            @pl.loop(2 * step - 2, 2 * step)
            def _(l):
                features(l)

        @pl.when(step == 2)
        def _():
            x_own.start()
            for copy in x_out:
                copy.start()

        @pl.when(step == 3)
        def _():
            x_own.wait()
            for copy in x_out:
                copy.wait()

        each(forward_done(step - 1), forward_done(step), forward)
        pass_on(1 - c)

        @pl.when(step == 4)
        def _():
            for k in order:
                cot_z(k).wait_recv()
                for n in range(3):
                    cot_x(1 - zh, k, n).start()

        @pl.when(step == 6)
        def _():
            for k in (0, 1):
                for half in (0, 1):
                    for n in range(3):
                        cot_x(half, k, n).wait_recv()

            @pl.loop(0, 4 * NX)
            def _(piece):
                for which in (0, 1):
                    at = pl.ds(pl.multiple_of(which * 256 + piece * 16, 16), 16)
                    value = cp[piece, 96 * which : 96 * which + 96].astype(F32)
                    for zs, rows16 in enumerate(spaced(value, NZ)):
                        cg[zs, at] = rows16

        each(backward_done(step - 1), backward_done(step), backward)
        each(forward_done(step - 2), forward_done(step - 1), collect)

        @pl.when(step >= NZ - 1)
        def _():
            each(jnp.where(step == NZ - 1, 0, forward_done(step - 2)), forward_done(step - 1), lambda zs: out_far(zs).start())

    def packed(k, which, lanes):
        tiles = []
        for m in range(8):
            at = pl.ds(pl.multiple_of(which * 256 + 32 * m, 32), 32)
            tiles += dense(acc[k, at, lanes])
        return jnp.concatenate(tiles, axis=0)

    g_out = [
        remote(gsend.at[n], grecv.at[n], g_s.at[n], g_r.at[n], to)
        for n, to in enumerate((part_same, part_other, sib))
    ]
    for n, (k, which) in enumerate(((c, 1 - t), (1 - c, 1 - t), (1 - c, t))):
        for l in range(4):
            lanes = slice(l * 128, (l + 1) * 128)
            gsend[n, :, lanes] = packed(k, which, lanes).astype(BF16)
        g_out[n].start()

    for copy in g_out:
        copy.wait()

    def gradients(l):
        lanes = lane(l)
        mixed_grad = packed(c, t, lanes)
        for n in range(3):
            mixed_grad = mixed_grad + grecv[n, :, lanes].astype(F32)
        long_grad = mixed_grad * qf[:, lanes]
        query_grad = mixed_grad * ls[:, lanes]
        glb[:T, lanes] = long_grad
        gq[:, lanes] = query_grad
        head[:128, lanes] = long_grad[:128].astype(BF16)
        head[128:, lanes] = query_grad[:TAIL].astype(BF16)

    @pl.loop(0, 4)
    def _(l):
        gradients(l)

    head_copy = remote(head, head_in, h_s.at[3], h_r.at[3], prv)

    @pl.when(ctx > 0)
    def _():
        head_copy.start()

    @pl.loop(0, 4)
    def _(l):
        lanes = lane(l)
        grad = glb[:T, lanes]

        @pl.loop(0, 8)
        def _(r):
            for q in range(16):
                total[r, q : q + 1, lanes] = jnp.sum(
                    grad * rot[r, pl.ds(PRE - 8 * q, T), lanes], axis=0, keepdims=True
                )

        for t in range(8):
            part[l, t] = total[t, :, lanes].astype(BF16)

    def to_y(n):
        return remote(part.at[(y + n + 1) % NY], ybuf.at[n], py_s.at[n], py_r.at[n], ys[n])

    def taps_y(n):
        return remote(tpart.at[(y + n + 1) % NY], tybuf.at[n], ty_s.at[n], ty_r.at[n], ys[n])

    def to_z(n):
        return remote(mine.at[(zl + n + 1) % NZ], zbuf.at[n], pz_s.at[n], pz_r.at[n], zs_all[n])

    def taps_z(n):
        return remote(tmine, tzbuf.at[n], pt_s.at[n], pt_r.at[n], zs_all[n])

    def back_z(n):
        return remote(other.at[y, zl], other.at[y, zl], bz_s.at[n], bz_r.at[n], zs_all[n])

    def back_y(n):
        return remote(other.at[y], other.at[y], by_s.at[n], by_r.at[n], ys[n])

    for n in range(3):
        to_y(n).start()

    def finish(zs):
        collect(zs)
        out_far(zs).start()

    each(forward_done(NZ - 1), NZ, finish)

    @pl.when(ctx < last_ctx)
    def _():
        head_copy.wait_recv()

    @pl.loop(0, 4)
    def _(l):
        lanes = lane(l)
        glb[T:, lanes] = head_in[:128, lanes].astype(F32)
        full = glb[:, lanes]
        rg[0] = full
        for r in range(1, 8):
            rg[r] = pltpu.roll(full, full.shape[0] - r, 0)
        pair_grad = convolve(lambda r, at: rg[r, pl.ds(at, T)], 0, 1, lanes)
        key_grad = pair_grad * vf[:, lanes]
        value_grad = pair_grad * kf[:, lanes]
        gk[:, lanes] = key_grad
        gv[:, lanes] = value_grad
        lead[0, :, lanes] = key_grad[:TAIL].astype(BF16)
        lead[1, :, lanes] = value_grad[:TAIL].astype(BF16)
        for b, (at, grad) in enumerate(
            ((0, gq[:, lanes]), (PRE, key_grad), (2 * PRE, value_grad))
        ):
            raw = jnp.concatenate(
                [halo[at : at + TAIL, lanes].astype(F32), br_ref[b, :, lanes].astype(F32)], axis=0
            )
            for i in range(3):
                moved = raw if i == 0 else pltpu.roll(raw, i, 0)
                tg[3 * b + i : 3 * b + i + 1, lanes] = jnp.sum(grad * moved[TAIL:], axis=0, keepdims=True)
        tpart[l] = tg[:, lanes].astype(BF16)

    lead_copy = remote(lead, lead_in, h_s.at[4], h_r.at[4], prv)

    @pl.when(ctx > 0)
    def _():
        lead_copy.start()

    for n in range(3):
        taps_y(n).start()

    value = part[y].astype(F32)
    for n in range(3):
        to_y(n).wait_recv()
        value = value + ybuf[n].astype(F32)
    mine[...] = value.astype(BF16)
    for n in range(NZ - 1):
        to_z(n).start()

    value = tpart[y].astype(F32)
    for n in range(3):
        taps_y(n).wait_recv()
        value = value + tybuf[n].astype(F32)
    tmine[...] = value.astype(BF16)
    for n in range(NZ - 1):
        taps_z(n).start()

    @pl.when(ctx < last_ctx)
    def _():
        lead_copy.wait_recv()

    @pl.loop(0, 4)
    def _(l):
        lanes = lane(l)
        for b, (grad, ahead) in enumerate(
            ((gq, head_in[128:, lanes]), (gk, lead_in[0, :, lanes]), (gv, lead_in[1, :, lanes]))
        ):
            full = jnp.concatenate([grad[:, lanes], ahead.astype(F32)], axis=0)
            value = taps_ref[b, 0:1, lanes] * full
            for i in (1, 2):
                value = value + taps_ref[b, i : i + 1, lanes] * pltpu.roll(full, T + TAIL - i, 0)
            gin_ref[b, :, lanes] = value[:T].astype(BF16)

    value = mine[zl].astype(F32)
    for n in range(NZ - 1):
        to_z(n).wait_recv()
        value = value + zbuf[n].astype(F32)
    other[y, zl] = value.astype(BF16)
    for n in range(NZ - 1):
        back_z(n).start()

    for zs in range(NZ):
        out_far(zs).wait()
        value = sums[zh, zs].astype(F32) + far[zs].astype(F32)
        for which in (0, 1):
            for k, rows16 in enumerate(spaced(value[24 * which : 24 * which + 24], 2)):
                near[which, k, zs] = rows16
    m_out = [
        remote(near.at[which, k], come.at[ps, c], m_s.at[n], m_r.at[n], to)
        for n, (which, k, to) in enumerate(
            ((t, 1 - c, sib), (1 - t, c, part_same), (1 - t, 1 - c, part_other))
        )
    ]
    for copy in m_out:
        copy.start()
    come[ps, c] = near[t, c]

    value = tmine[...].astype(F32)
    for n in range(NZ - 1):
        taps_z(n).wait_recv()
        value = value + tzbuf[n].astype(F32)
    other[y, NZ] = value.astype(BF16)
    for n in range(NZ - 1):
        back_z(n).wait()
    for n in range(3):
        back_y(n).start()
    for copy in m_out:
        copy.wait()
    for p, both_y in enumerate(((0, 3), (1, 2))):
        for k in (0, 1):
            for zs in range(NZ):
                for j, yy in enumerate(both_y):
                    at = (zs * NY + yy) * 256 + k * 128
                    mixed_ref[:, at : at + 128] = come[p, k, zs, :, j * 128 : (j + 1) * 128][:12]

    for n in range(3):
        back_y(n).wait()
    for l in range(4):
        for t in range(8):
            total[t, :, l * 128 : (l + 1) * 128] = other[l, t].astype(F32)
        tg[:, l * 128 : (l + 1) * 128] = other[l, NZ].astype(F32)
    for j in range(128):
        gfil_ref[j : j + 1] = total[j % 8, j // 8 : j // 8 + 1]
    for b in range(3):
        gtap_ref[b] = tg[3 * b : 3 * b + 3]
    for n in range(3):
        to_y(n).wait_send()
        taps_y(n).wait_send()
    for n in range(NZ - 1):
        to_z(n).wait_send()
        taps_z(n).wait_send()

    @pl.when(ctx > 0)
    def _():
        head_copy.wait_send()
        lead_copy.wait_send()

    @pl.when(ctx < last_ctx)
    def _():
        for copy in halo_copies:
            copy.wait_send()

    @pl.loop(0, NZ)
    def _(zs):
        for h in (0, 1):
            across(zs, js, h).wait_send()

            @pl.when((zs <= zl) & (zl < NZ - 1))
            def _():
                z_right(zs, h).wait_send()

            @pl.when((zs >= zl) & (zl > 0))
            def _():
                z_left(zs, h).wait_send()

        for n in range(3):
            out_x(zs, n).wait_send()

    for copy in c_pair:
        copy.wait_send()
    for k in (0, 1):
        cot_z(k).wait_send()
        for half in (0, 1):
            for n in range(3):
                cot_x(half, k, n).wait_send()


def block(branches, taps, filt, weight, cot):
    rows = weight.shape[0]
    wide = branches.shape[2]
    dma = pltpu.SemaphoreType.DMA
    vmem = pl.BlockSpec(memory_space=pltpu.VMEM)

    def f32(*shape):
        return pltpu.VMEM(shape, F32)

    def b16(*shape):
        return pltpu.VMEM(shape, BF16)

    return pl.pallas_call(
        block_kernel,
        out_shape=(
            jax.ShapeDtypeStruct((12, 8192), BF16),
            jax.ShapeDtypeStruct(branches.shape, BF16),
            jax.ShapeDtypeStruct(filt.shape, F32),
            jax.ShapeDtypeStruct(taps.shape, F32),
        ),
        in_specs=[vmem] * 5,
        out_specs=(vmem,) * 4,
        scratch_shapes=[
            b16(16, cot.shape[1]), b16(2, 2, 96, 256), f32(*taps.shape), f32(8, 16, wide),
            b16(NZ * 2, 2 * rows, 128), b16(4 * NX, 192, 256), b16(NZ, 512, 256), b16(TAIL + 2 * PRE, wide),
            f32(T, wide), f32(T, wide), f32(T, wide), f32(T, wide), f32(8, T + PRE, wide),
            b16(256, wide), b16(2, 512, wide), f32(2, 512, wide),
            b16(NZ, NX, 96, 256), b16(NZ, 3, 96, 256), b16(3, T, wide), b16(3, T, wide),
            b16(2, NZ, 48, 256), b16(NZ, 48, 256), b16(2, 2, NZ, 16, 256), b16(2, 2, NZ, 16, 256),
            b16(NY, NZ + 1, 16, 128),
            f32(T + 128, wide), f32(8, T + 128, 128), f32(T, wide), f32(T, wide), f32(T, wide),
            b16(128 + TAIL, wide), b16(128 + TAIL, wide), b16(2, TAIL, wide), b16(2, TAIL, wide), f32(16, wide),
            b16(NY, NZ, 16, 128), b16(NZ, 16, 128), b16(3, NZ, 16, 128), b16(NZ - 1, 16, 128), f32(8, 16, wide),
            b16(NY, 16, 128), b16(16, 128), b16(3, 16, 128), b16(NZ - 1, 16, 128),
            dma((3,)), dma((2,)), dma((2,)), dma((2,)), dma((2,)), dma((3,)), dma((3,)), dma((3,)), dma((3,)), dma((3,)), dma((3,)),
            dma((2, NZ, 2)), dma((NZ, 2)), dma((NZ, 2)), dma((NZ, 2)),
            dma((2, 2, 3)), dma((2, 2, 3)), dma((NZ, 3)), dma((NZ, 3)), dma((2,)), dma((2,)), dma((NZ,)), dma((NZ,)), dma((5,)), dma((5,)),
            dma((3,)), dma((3,)), dma((NZ - 1,)), dma((NZ - 1,)), dma((NZ - 1,)), dma((NZ - 1,)),
            dma((NZ - 1,)), dma((NZ - 1,)), dma((3,)), dma((3,)), dma((3,)), dma((3,)),
        ],
        compiler_params=pltpu.CompilerParams(
            collective_id=0, has_side_effects=True, vmem_limit_bytes=56 * 2**20
        ),
        name="hyena_block",
    )(branches, taps, filt, weight, cot)


def body(branch_inputs, feat_taps, long_filter, out_weight, cotangent):
    return block(branch_inputs, feat_taps, long_filter, out_weight, cotangent)


def solution(mesh):
    placed = (
        P(None, "ctx", "tp"),
        P(None, None, "tp"),
        P(None, "tp"),
        P("tp", "ctx"),
        P(("ctx", "tp"), None),
    )
    return jax.shard_map(
        body,
        mesh=mesh,
        in_specs=placed,
        out_specs=(
            P(("ctx", "tp"), None),
            P(None, "ctx", "tp"),
            P(None, "tp"),
            P(None, None, "tp"),
        ),
        check_vma=False,
    )
```

```python
import functools

import jax
import jax.numpy as jnp
from jax import lax
from jax.experimental import pallas as pl
from jax.experimental.pallas import tpu as pltpu
from jax.sharding import PartitionSpec as P

MESH = pl.DeviceIdType.MESH
NZ, NY, NX = 8, 4, 4


def coords():
    ctx = lax.axis_index("ctx")
    tp = lax.axis_index("tp")
    return ctx, tp, ctx // NY, ctx % NY, tp // (2 * NX), (tp // 2) % NX, tp % 2


def device(zl, y, zh, x, c):
    return {"ctx": zl * NY + y, "tp": zh * (2 * NX) + x * 2 + c}


def remote(src, dst, send, recv, target):
    return pltpu.make_async_remote_copy(
        src_ref=src, dst_ref=dst, send_sem=send, recv_sem=recv, device_id=target, device_id_type=MESH
    )


def greet(targets):
    barrier = pltpu.get_barrier_semaphore()
    count = 0
    for target, there in targets:
        if there is True:
            pl.semaphore_signal(barrier, inc=1, device_id=target, device_id_type=MESH)
            count = count + 1
        else:
            @pl.when(there)
            def _():
                pl.semaphore_signal(barrier, inc=1, device_id=target, device_id_type=MESH)

            count = count + there.astype(jnp.int32)
    pl.semaphore_wait(barrier, count)


T = 192
PRE = 144
TAIL = 16
F32, BF16 = jnp.float32, jnp.bfloat16


def block_kernel(
    br_ref, ftaps_ref, filt_ref, w_ref, cot_in,
    mixed_ref, gin_ref, gfil_ref, gtap_ref,
    cot16, cot_ref, taps_ref, fil_ref, wg, cp, cg, halo, qf, kf, vf, ls, rot, gated, both, acc, out, arrived, gsend, grecv,
    sums, far, near, come, other, glb, rg, gq, gk, gv, head, head_in, lead, lead_in, tg,
    part, mine, ybuf, zbuf, total, tpart, tmine, tybuf, tzbuf,
    own_sem, sib_s, sib_r, cy_s, cy_r, xp_s, xp_r, g_s, g_r, m_s, m_r, z_s, z_r, y_s, y_r, x_s, x_r, o_s, o_r, zp_s, zp_r, f_s, f_r, h_s, h_r,
    py_s, py_r, pz_s, pz_r, pt_s, pt_r, bz_s, bz_r, by_s, by_r, ty_s, ty_r,
):
    ctx, tp, zl, y, zh, x, c = coords()
    t = y % 2
    yx, ps, js = y + 1 - 2 * t, ((y + 1) // 2) % 2, y // 2
    wy = device(zl, 3 - y, zh, x, c)
    part_same, part_other = device(zl, yx, zh, x, c), device(zl, yx, zh, x, 1 - c)
    sib = device(zl, y, zh, x, 1 - c)
    zpart = device(zl, y, 1 - zh, x, c)
    xs = [device(zl, y, zh, (x + k) % NX, c) for k in (1, 2, 3)]
    ys = [device(zl, (y + k) % NY, zh, x, c) for k in (1, 2, 3)]
    zs_all = [device((zl + k) % NZ, y, zh, x, c) for k in range(1, NZ)]
    dright = device(jnp.minimum(zl + 1, NZ - 1), y, zh, x, c)
    dleft = device(jnp.maximum(zl - 1, 0), y, zh, x, c)
    last_ctx = NZ * NY - 1
    nxt = {"ctx": jnp.minimum(ctx + 1, last_ctx), "tp": tp}
    prv = {"ctx": jnp.maximum(ctx - 1, 0), "tp": tp}
    greet(
        [(sib, True), (zpart, True), (part_other, True)]
        + [(d, True) for d in xs + ys + zs_all]
        + [(nxt, ctx < last_ctx), (prv, ctx > 0)]
    )
    rows = w_ref.shape[0]

    def unit(zs, j, h):
        return wg.at[zs * 2 + j, pl.ds(pl.multiple_of(h * rows, rows), rows)]

    def token_rows(which):
        return pl.ds(pl.multiple_of(which * 256, 256), 256)

    def cot_rows(which):
        return pl.ds(pl.multiple_of(which * 96, 96), 96)

    keep = w_ref.at[:, pl.ds(pl.multiple_of(c * 128, 128), 128)]
    give = w_ref.at[:, pl.ds(pl.multiple_of((1 - c) * 128, 128), 128)]
    w_sib = remote(give, unit(zl, js, c), sib_s.at[0], sib_r.at[0], sib)
    w_sib.start()
    w_own = pltpu.make_async_copy(keep, unit(zl, js, c), own_sem.at[0])
    w_own.start()
    halo_copies = [
        remote(br_ref.at[b, pl.ds(T - n, n)], halo.at[pl.ds(at, n)], h_s.at[b], h_r.at[b], nxt)
        for b, n, at in ((0, TAIL, 0), (1, PRE, TAIL), (2, PRE, TAIL + PRE))
    ]

    @pl.when(ctx < last_ctx)
    def _():
        for copy in halo_copies:
            copy.start()

    def dense(value):
        low = lax.broadcasted_iota(jnp.int32, (8, value.shape[1]), 0) < 4
        up, down = pltpu.roll(value[16:24], 4, 0), pltpu.roll(value[24:32], 4, 0)
        return [value[:8], jnp.where(low, value[8:16], up), jnp.where(low, up, down)]

    cot16[...] = jnp.zeros_like(cot16)
    cot16[:12] = cot_in[...]
    for p, both_y in enumerate(((0, 3), (1, 2))):
        for k in (0, 1):
            for j, yy in enumerate(both_y):
                tiles = []
                for m in range(NZ // 2):
                    pair = [
                        cot16[:, pl.ds(((2 * m + n) * NY + yy) * 256 + k * 128, 128)].astype(F32) for n in (0, 1)
                    ]
                    tiles += dense(jnp.concatenate(pair, axis=0))
                cot_ref[p, k, :, j * 128 : (j + 1) * 128] = jnp.concatenate(tiles, axis=0).astype(BF16)
    c_here = cp.at[tp, cot_rows(t)]
    c_sib = remote(cot_ref.at[ps, 1 - c], c_here, sib_s.at[1], sib_r.at[1], sib)
    c_pair = [
        remote(cot_ref.at[1 - ps, c], c_here, cy_s.at[0], cy_r.at[0], part_same),
        remote(cot_ref.at[1 - ps, 1 - c], c_here, cy_s.at[1], cy_r.at[1], part_other),
    ]
    c_own = pltpu.make_async_copy(cot_ref.at[ps, c], c_here, own_sem.at[1])
    for copy in [c_sib, c_own] + c_pair:
        copy.start()
    def z_right(zs, h):
        return remote(unit(zs, js, h), unit(zs, js, h), z_s.at[0, zs, h], z_r.at[zs, h], dright)

    def z_left(zs, h):
        return remote(unit(zs, js, h), unit(zs, js, h), z_s.at[1, zs, h], z_r.at[zs, h], dleft)

    def across(zs, j, h):
        return remote(unit(zs, j, h), unit(zs, j, h), y_s.at[zs, h], y_r.at[zs, h], wy)

    def spread(zs, h):
        across(zs, js, h).start()

    def cot_z(k):
        piece = zh * (2 * NX) + x * 2 + k
        return remote(cp.at[piece], cp.at[piece], zp_s.at[k], zp_r.at[k], zpart)

    def cot_x(half, k, n):
        piece = half * (2 * NX) + x * 2 + k
        return remote(cp.at[piece], cp.at[piece], x_s.at[half, k, n], x_r.at[half, k, n], xs[n])

    def out_x(zs, n):
        return remote(out.at[zs, (x + n + 1) % NX], arrived.at[zs, n], o_s.at[zs, n], o_r.at[zs, n], xs[n])

    order = (c, 1 - c)
    w_own.wait()
    for h in order:
        if h is not c:
            w_sib.wait()

        @pl.when(zl < NZ - 1)
        def _(h=h):
            z_right(zl, h).start()

        @pl.when(zl > 0)
        def _(h=h):
            z_left(zl, h).start()

        spread(zl, h)
        if h is c:
            c_own.wait()
            c_pair[0].wait_recv()
        else:
            c_sib.wait()
            c_pair[1].wait_recv()
        cot_z(h).start()
        for n in range(3):
            cot_x(zh, h, n).start()
    for b in range(3):
        taps_ref[b] = ftaps_ref[b].astype(F32)
    for j in range(128):
        fil_ref[j % 8, j // 8 : j // 8 + 1] = filt_ref[j : j + 1]
    acc[...] = jnp.zeros_like(acc)
    tg[...] = jnp.zeros_like(tg)

    @pl.when(ctx == 0)
    def _():
        halo[...] = jnp.zeros_like(halo)

    @pl.when(ctx == last_ctx)
    def _():
        head_in[...] = jnp.zeros_like(head_in)
        lead_in[...] = jnp.zeros_like(lead_in)

    def lane(l):
        return pl.ds(pl.multiple_of(l * 128, 128), 128)

    def spaced(value, count):
        shifted = pltpu.roll(value, value.shape[0] - 4, 0)
        for i in range(count):
            at = 12 * i
            yield (value[at : at + 16] if at % 8 == 0 else shifted[at - 4 : at + 12]).astype(BF16)

    def convolve(source, first, step, lanes):
        def residue(r, value):
            for q in range(16):
                tap = fil_ref[r, q : q + 1, lanes]
                value = value + tap * source(r, first + step * 8 * q)
            return value

        return lax.fori_loop(0, 8, residue, jnp.zeros((T, 128), F32))

    def features(l):
        lanes = lane(l)

        def feature(b, at, n):
            raw = jnp.concatenate([halo[at : at + n, lanes].astype(F32), br_ref[b, :, lanes].astype(F32)], axis=0)
            value = taps_ref[b, 0:1, lanes] * raw
            for i in (1, 2):
                value = value + taps_ref[b, i : i + 1, lanes] * pltpu.roll(raw, i, 0)
            return value.astype(BF16).astype(F32)

        query = feature(0, 0, TAIL)[TAIL:]
        key = feature(1, TAIL, PRE)
        value = feature(2, TAIL + PRE, PRE)
        qf[:, lanes] = query
        kf[:, lanes] = key[PRE:]
        vf[:, lanes] = value[PRE:]
        pair = (key * value).astype(BF16).astype(F32)
        rot[0, :, lanes] = pair
        for r in range(1, 8):
            rot[r, :, lanes] = pltpu.roll(pair, r, 0)
        long = convolve(lambda r, at: rot[r, pl.ds(at, T), lanes], PRE, -1, lanes)
        ls[:, lanes] = long
        for i, rows16 in enumerate(spaced(query * long, 16)):
            gated[16 * i : 16 * i + 16, lanes] = rows16

    def weight(zs, k):
        return jnp.concatenate([wg[zs * 2 + j, k * rows : (k + 1) * rows] for j in (0, 1)], axis=1)

    def forward(zs):
        value = jnp.dot(both[0], weight(zs, 0), preferred_element_type=F32)
        value = value + jnp.dot(both[1], weight(zs, 1), preferred_element_type=F32)
        for xx in range(NX):
            groups = []
            for which in (0, 1):
                for half in (0, 1):
                    at = which * 256 + (half * NX + xx) * 32
                    groups += dense(value[at : at + 32])
            out[zs, xx] = jnp.concatenate(groups, axis=0).astype(BF16)
        for n in range(3):
            out_x(zs, n).start()

    def backward(zs):
        for k in (0, 1):
            acc[k] += lax.dot_general(
                cg[zs], weight(zs, k), (((1,), (1,)), ((), ())), preferred_element_type=F32
            )

    def collect(zs):
        value = out[zs, x].astype(F32)
        for n in range(3):
            out_x(zs, n).wait_recv()
            value = value + arrived[zs, n].astype(F32)
        for half in (0, 1):
            at = 24 * half
            sums[half, zs] = jnp.concatenate([value[at : at + 24], value[48 + at : 72 + at]], axis=0).astype(BF16)

    def out_far(zs):
        return remote(sums.at[1 - zh, zs], far.at[zs], f_s.at[zs], f_r.at[zs], zpart)

    near_end = jnp.minimum(zl, NZ - 1 - zl)

    def nth(n):
        paired = jnp.where(n % 2 == 1, zl - (n + 1) // 2, zl + n // 2)
        single = jnp.where(zl < NZ // 2, zl + (n - near_end), zl - (n - near_end))
        return jnp.where(n <= 2 * near_end, paired, single)

    def each(first, last, act):
        @pl.loop(first, last)
        def _(n):
            act(nth(n))

    x_here = both.at[c, token_rows(t)]
    x_out = [
        remote(gated, x_here, xp_s.at[n], xp_r.at[n], to) for n, to in enumerate((sib, part_same, part_other))
    ]
    x_own = pltpu.make_async_copy(gated, x_here, own_sem.at[2])

    def forward_done(step):
        return jnp.maximum(0, jnp.minimum(2 * (step - 4), step))

    def backward_done(step):
        return jnp.maximum(0, jnp.minimum(3 * (step - 5), step))

    @pl.loop(1, NZ + 1)
    def _(step):
        def pass_on(h):
            @pl.when(zl - step >= 0)
            def _():
                z_right(zl - step, h).wait_recv()

                @pl.when(zl < NZ - 1)
                def _():
                    z_right(zl - step, h).start()

            @pl.when(zl + step < NZ)
            def _():
                z_left(zl + step, h).wait_recv()

                @pl.when(zl > 0)
                def _():
                    z_left(zl + step, h).start()

            @pl.when(step < NZ)
            def _():
                spread(nth(step), h)

        pass_on(c)
        for h in order:
            across(nth(step - 1), 1 - js, h).wait_recv()

        @pl.when((step == 1) & (ctx > 0))
        def _():
            for copy in halo_copies:
                copy.wait_recv()

        @pl.when(step <= 4)
        def _():
            features(step - 1)

        @pl.when(step == 4)
        def _():
            x_own.start()
            for copy in x_out:
                copy.start()

        @pl.when(step == 5)
        def _():
            x_own.wait()
            for copy in x_out:
                copy.wait()

        each(forward_done(step - 1), forward_done(step), forward)
        pass_on(1 - c)

        @pl.when(step == 4)
        def _():
            for k in order:
                cot_z(k).wait_recv()
                for n in range(3):
                    cot_x(1 - zh, k, n).start()

        @pl.when(step == 6)
        def _():
            for k in (0, 1):
                for half in (0, 1):
                    for n in range(3):
                        cot_x(half, k, n).wait_recv()

            @pl.loop(0, 4 * NX)
            def _(piece):
                for which in (0, 1):
                    at = pl.ds(pl.multiple_of(which * 256 + piece * 16, 16), 16)
                    value = cp[piece, 96 * which : 96 * which + 96].astype(F32)
                    for zs, rows16 in enumerate(spaced(value, NZ)):
                        cg[zs, at] = rows16

        each(backward_done(step - 1), backward_done(step), backward)
        each(forward_done(step - 2), forward_done(step - 1), collect)

        @pl.when(step >= NZ - 1)
        def _():
            each(jnp.where(step == NZ - 1, 0, forward_done(step - 2)), forward_done(step - 1), lambda zs: out_far(zs).start())

    def packed(k, which, lanes):
        tiles = []
        for m in range(8):
            at = pl.ds(pl.multiple_of(which * 256 + 32 * m, 32), 32)
            tiles += dense(acc[k, at, lanes])
        return jnp.concatenate(tiles, axis=0)

    g_out = [
        remote(gsend.at[n], grecv.at[n], g_s.at[n], g_r.at[n], to)
        for n, to in enumerate((part_same, part_other, sib))
    ]
    for n, (k, which) in enumerate(((c, 1 - t), (1 - c, 1 - t), (1 - c, t))):
        for l in range(4):
            lanes = slice(l * 128, (l + 1) * 128)
            gsend[n, :, lanes] = packed(k, which, lanes).astype(BF16)
        g_out[n].start()

    for copy in g_out:
        copy.wait()

    def gradients(l):
        lanes = lane(l)
        mixed_grad = packed(c, t, lanes)
        for n in range(3):
            mixed_grad = mixed_grad + grecv[n, :, lanes].astype(F32)
        long_grad = mixed_grad * qf[:, lanes]
        query_grad = mixed_grad * ls[:, lanes]
        glb[:T, lanes] = long_grad
        gq[:, lanes] = query_grad
        head[:128, lanes] = long_grad[:128].astype(BF16)
        head[128:, lanes] = query_grad[:TAIL].astype(BF16)

    @pl.loop(0, 4)
    def _(l):
        gradients(l)

    head_copy = remote(head, head_in, h_s.at[3], h_r.at[3], prv)

    @pl.when(ctx > 0)
    def _():
        head_copy.start()

    @pl.loop(0, 4)
    def _(l):
        lanes = lane(l)
        grad = glb[:T, lanes]

        @pl.loop(0, 8)
        def _(r):
            for q in range(16):
                total[r, q : q + 1, lanes] = jnp.sum(
                    grad * rot[r, pl.ds(PRE - 8 * q, T), lanes], axis=0, keepdims=True
                )

        for t in range(8):
            part[l, t] = total[t, :, lanes].astype(BF16)

    def to_y(n):
        return remote(part.at[(y + n + 1) % NY], ybuf.at[n], py_s.at[n], py_r.at[n], ys[n])

    def taps_y(n):
        return remote(tpart.at[(y + n + 1) % NY], tybuf.at[n], ty_s.at[n], ty_r.at[n], ys[n])

    def to_z(n):
        return remote(mine.at[(zl + n + 1) % NZ], zbuf.at[n], pz_s.at[n], pz_r.at[n], zs_all[n])

    def taps_z(n):
        return remote(tmine, tzbuf.at[n], pt_s.at[n], pt_r.at[n], zs_all[n])

    def back_z(n):
        return remote(other.at[y, zl], other.at[y, zl], bz_s.at[n], bz_r.at[n], zs_all[n])

    def back_y(n):
        return remote(other.at[y], other.at[y], by_s.at[n], by_r.at[n], ys[n])

    for n in range(3):
        to_y(n).start()

    def finish(zs):
        collect(zs)
        out_far(zs).start()

    each(forward_done(NZ - 1), NZ, finish)

    @pl.when(ctx < last_ctx)
    def _():
        head_copy.wait_recv()

    @pl.loop(0, 4)
    def _(l):
        lanes = lane(l)
        glb[T:, lanes] = head_in[:128, lanes].astype(F32)
        full = glb[:, lanes]
        rg[0] = full
        for r in range(1, 8):
            rg[r] = pltpu.roll(full, full.shape[0] - r, 0)
        pair_grad = convolve(lambda r, at: rg[r, pl.ds(at, T)], 0, 1, lanes)
        key_grad = pair_grad * vf[:, lanes]
        value_grad = pair_grad * kf[:, lanes]
        gk[:, lanes] = key_grad
        gv[:, lanes] = value_grad
        lead[0, :, lanes] = key_grad[:TAIL].astype(BF16)
        lead[1, :, lanes] = value_grad[:TAIL].astype(BF16)
        for b, (at, grad) in enumerate(
            ((0, gq[:, lanes]), (PRE, key_grad), (2 * PRE, value_grad))
        ):
            raw = jnp.concatenate(
                [halo[at : at + TAIL, lanes].astype(F32), br_ref[b, :, lanes].astype(F32)], axis=0
            )
            for i in range(3):
                moved = raw if i == 0 else pltpu.roll(raw, i, 0)
                tg[3 * b + i : 3 * b + i + 1, lanes] = jnp.sum(grad * moved[TAIL:], axis=0, keepdims=True)
        tpart[l] = tg[:, lanes].astype(BF16)

    lead_copy = remote(lead, lead_in, h_s.at[4], h_r.at[4], prv)

    @pl.when(ctx > 0)
    def _():
        lead_copy.start()

    for n in range(3):
        taps_y(n).start()

    value = part[y].astype(F32)
    for n in range(3):
        to_y(n).wait_recv()
        value = value + ybuf[n].astype(F32)
    mine[...] = value.astype(BF16)
    for n in range(NZ - 1):
        to_z(n).start()

    value = tpart[y].astype(F32)
    for n in range(3):
        taps_y(n).wait_recv()
        value = value + tybuf[n].astype(F32)
    tmine[...] = value.astype(BF16)
    for n in range(NZ - 1):
        taps_z(n).start()

    @pl.when(ctx < last_ctx)
    def _():
        lead_copy.wait_recv()

    @pl.loop(0, 4)
    def _(l):
        lanes = lane(l)
        for b, (grad, ahead) in enumerate(
            ((gq, head_in[128:, lanes]), (gk, lead_in[0, :, lanes]), (gv, lead_in[1, :, lanes]))
        ):
            full = jnp.concatenate([grad[:, lanes], ahead.astype(F32)], axis=0)
            value = taps_ref[b, 0:1, lanes] * full
            for i in (1, 2):
                value = value + taps_ref[b, i : i + 1, lanes] * pltpu.roll(full, T + TAIL - i, 0)
            gin_ref[b, :, lanes] = value[:T].astype(BF16)

    value = mine[zl].astype(F32)
    for n in range(NZ - 1):
        to_z(n).wait_recv()
        value = value + zbuf[n].astype(F32)
    other[y, zl] = value.astype(BF16)
    for n in range(NZ - 1):
        back_z(n).start()

    for zs in range(NZ):
        out_far(zs).wait()
        value = sums[zh, zs].astype(F32) + far[zs].astype(F32)
        for which in (0, 1):
            for k, rows16 in enumerate(spaced(value[24 * which : 24 * which + 24], 2)):
                near[which, k, zs] = rows16
    m_out = [
        remote(near.at[which, k], come.at[ps, c], m_s.at[n], m_r.at[n], to)
        for n, (which, k, to) in enumerate(
            ((t, 1 - c, sib), (1 - t, c, part_same), (1 - t, 1 - c, part_other))
        )
    ]
    for copy in m_out:
        copy.start()
    come[ps, c] = near[t, c]

    value = tmine[...].astype(F32)
    for n in range(NZ - 1):
        taps_z(n).wait_recv()
        value = value + tzbuf[n].astype(F32)
    other[y, NZ] = value.astype(BF16)
    for n in range(NZ - 1):
        back_z(n).wait()
    for n in range(3):
        back_y(n).start()
    for copy in m_out:
        copy.wait()
    for p, both_y in enumerate(((0, 3), (1, 2))):
        for k in (0, 1):
            for zs in range(NZ):
                for j, yy in enumerate(both_y):
                    at = (zs * NY + yy) * 256 + k * 128
                    mixed_ref[:, at : at + 128] = come[p, k, zs, :, j * 128 : (j + 1) * 128][:12]

    for n in range(3):
        back_y(n).wait()
    for l in range(4):
        for t in range(8):
            total[t, :, l * 128 : (l + 1) * 128] = other[l, t].astype(F32)
        tg[:, l * 128 : (l + 1) * 128] = other[l, NZ].astype(F32)
    for j in range(128):
        gfil_ref[j : j + 1] = total[j % 8, j // 8 : j // 8 + 1]
    for b in range(3):
        gtap_ref[b] = tg[3 * b : 3 * b + 3]
    for n in range(3):
        to_y(n).wait_send()
        taps_y(n).wait_send()
    for n in range(NZ - 1):
        to_z(n).wait_send()
        taps_z(n).wait_send()

    @pl.when(ctx > 0)
    def _():
        head_copy.wait_send()
        lead_copy.wait_send()

    @pl.when(ctx < last_ctx)
    def _():
        for copy in halo_copies:
            copy.wait_send()

    @pl.loop(0, NZ)
    def _(zs):
        for h in (0, 1):
            across(zs, js, h).wait_send()

            @pl.when((zs <= zl) & (zl < NZ - 1))
            def _():
                z_right(zs, h).wait_send()

            @pl.when((zs >= zl) & (zl > 0))
            def _():
                z_left(zs, h).wait_send()

        for n in range(3):
            out_x(zs, n).wait_send()

    for copy in c_pair:
        copy.wait_send()
    for k in (0, 1):
        cot_z(k).wait_send()
        for half in (0, 1):
            for n in range(3):
                cot_x(half, k, n).wait_send()


def block(branches, taps, filt, weight, cot):
    rows = weight.shape[0]
    wide = branches.shape[2]
    dma = pltpu.SemaphoreType.DMA
    vmem = pl.BlockSpec(memory_space=pltpu.VMEM)

    def f32(*shape):
        return pltpu.VMEM(shape, F32)

    def b16(*shape):
        return pltpu.VMEM(shape, BF16)

    return pl.pallas_call(
        block_kernel,
        out_shape=(
            jax.ShapeDtypeStruct((12, 8192), BF16),
            jax.ShapeDtypeStruct(branches.shape, BF16),
            jax.ShapeDtypeStruct(filt.shape, F32),
            jax.ShapeDtypeStruct(taps.shape, F32),
        ),
        in_specs=[vmem] * 5,
        out_specs=(vmem,) * 4,
        scratch_shapes=[
            b16(16, cot.shape[1]), b16(2, 2, 96, 256), f32(*taps.shape), f32(8, 16, wide),
            b16(NZ * 2, 2 * rows, 128), b16(4 * NX, 192, 256), b16(NZ, 512, 256), b16(TAIL + 2 * PRE, wide),
            f32(T, wide), f32(T, wide), f32(T, wide), f32(T, wide), f32(8, T + PRE, wide),
            b16(256, wide), b16(2, 512, wide), f32(2, 512, wide),
            b16(NZ, NX, 96, 256), b16(NZ, 3, 96, 256), b16(3, T, wide), b16(3, T, wide),
            b16(2, NZ, 48, 256), b16(NZ, 48, 256), b16(2, 2, NZ, 16, 256), b16(2, 2, NZ, 16, 256),
            b16(NY, NZ + 1, 16, 128),
            f32(T + 128, wide), f32(8, T + 128, 128), f32(T, wide), f32(T, wide), f32(T, wide),
            b16(128 + TAIL, wide), b16(128 + TAIL, wide), b16(2, TAIL, wide), b16(2, TAIL, wide), f32(16, wide),
            b16(NY, NZ, 16, 128), b16(NZ, 16, 128), b16(3, NZ, 16, 128), b16(NZ - 1, 16, 128), f32(8, 16, wide),
            b16(NY, 16, 128), b16(16, 128), b16(3, 16, 128), b16(NZ - 1, 16, 128),
            dma((3,)), dma((2,)), dma((2,)), dma((2,)), dma((2,)), dma((3,)), dma((3,)), dma((3,)), dma((3,)), dma((3,)), dma((3,)),
            dma((2, NZ, 2)), dma((NZ, 2)), dma((NZ, 2)), dma((NZ, 2)),
            dma((2, 2, 3)), dma((2, 2, 3)), dma((NZ, 3)), dma((NZ, 3)), dma((2,)), dma((2,)), dma((NZ,)), dma((NZ,)), dma((5,)), dma((5,)),
            dma((3,)), dma((3,)), dma((NZ - 1,)), dma((NZ - 1,)), dma((NZ - 1,)), dma((NZ - 1,)),
            dma((NZ - 1,)), dma((NZ - 1,)), dma((3,)), dma((3,)), dma((3,)), dma((3,)),
        ],
        compiler_params=pltpu.CompilerParams(
            collective_id=0, has_side_effects=True, vmem_limit_bytes=56 * 2**20
        ),
        name="hyena_block",
    )(branches, taps, filt, weight, cot)


def body(branch_inputs, feat_taps, long_filter, out_weight, cotangent):
    return block(branch_inputs, feat_taps, long_filter, out_weight, cotangent)


def solution(mesh):
    placed = (
        P(None, "ctx", "tp"),
        P(None, None, "tp"),
        P(None, "tp"),
        P("tp", "ctx"),
        P(("ctx", "tp"), None),
    )
    return jax.shard_map(
        body,
        mesh=mesh,
        in_specs=placed,
        out_specs=(
            P(("ctx", "tp"), None),
            P(None, "ctx", "tp"),
            P(None, "tp"),
            P(None, None, "tp"),
        ),
        check_vma=False,
    )
```
